32 devices in a mesh: dp: 16 (over z, x, core), tensor: 2 (over y).
Axes of the slice: x: 2, y: 2, z: 4, core: 2. Of those that a mesh axis runs over, the one named last changes fastest.
Arguments:
- inputs: bfloat16 [16384, 1024], P('dp'), may hold values from -6 to 6
- lengths: int32 [16], P('dp'), may hold values from 256 to 1024, as said below
- gain_attn: bfloat16 [1024], replicated, may hold values from 0.5 to 1.5
- w_query: bfloat16 [1024, 1024], P(None, 'tensor'), may hold values from -0.1875 to 0.1875
- w_key: bfloat16 [1024, 1024], P(None, 'tensor'), may hold values from -0.1875 to 0.1875
- w_value: bfloat16 [1024, 1024], P(None, 'tensor'), may hold values from -0.1875 to 0.1875
- w_gate_attn: bfloat16 [1024, 1024], P(None, 'tensor'), may hold values from -0.1875 to 0.1875
- w_out: bfloat16 [1024, 1024], P('tensor'), may hold values from -0.25 to 0.25
- gain_ffn: bfloat16 [1024], replicated, may hold values from 0.5 to 1.5
- w_gate: bfloat16 [1024, 2816], P(None, 'tensor'), may hold values from -0.1875 to 0.1875
- w_up: bfloat16 [1024, 2816], P(None, 'tensor'), may hold values from -0.1875 to 0.1875
- w_down: bfloat16 [2816, 1024], P('tensor'), may hold values from -0.15625 to 0.15625
- cotangent: bfloat16 [16384, 1024], P('dp'), may hold values from -6 to 6
Outputs:
- result: bfloat16 [16384, 1024], P('dp')
- input_grad: bfloat16 [16384, 1024], P('dp')
- grad_gain_attn: float32 [1024], P('dp')
- grad_query: float32 [1024, 1024], P('dp', 'tensor')
- grad_key: float32 [1024, 1024], P('dp', 'tensor')
- grad_value: float32 [1024, 1024], P('dp', 'tensor')
- grad_gate_attn: float32 [1024, 1024], P('dp', 'tensor')
- grad_out: float32 [1024, 1024], P('tensor', 'dp')
- grad_gain_ffn: float32 [1024], P('dp')
- grad_gate: float32 [1024, 2816], P('dp', 'tensor')
- grad_up: float32 [1024, 2816], P('dp', 'tensor')
- grad_down: float32 [2816, 1024], P('tensor', 'dp')
The draws below stay inside these ranges and needn't reach their ends.
Inputs may be any that keep to these rules, and one draw needn't show every extreme that they name: Each sequence occupies 1024 slots of which its first lengths are live; some sequence fills all 1024.
All inputs are finite; a program needn't handle non-finite values.
Results may differ from the reference program's by a relative error of at most 0.02.
Values sent between devices are 32-bit elements; how exact they have to be, the bound alone decides.
No kernel may reach another device: no remote copies, remote signals or barrier semaphores. Data moves between devices by JAX's collectives and lax.ppermute only.
A program may use at most 256 MiB of HBM per device.

```python
import jax
import jax.numpy as jnp
from jax import lax

D = 1024
HEADS = 16
HEAD_DIM = 64
FF = 2816
SEQ_LEN = 1024
BLOCK = 512
SEQS = 16
TOKENS = 16384


def draw_lengths(key, part):
    key = jax.random.fold_in(key, 5)
    first_key, second_key = jax.random.split(key)
    drawn = jax.random.randint(first_key, (SEQS,), SEQ_LEN // 4, SEQ_LEN + 1)
    chosen = jax.random.randint(second_key, (), 0, SEQS)
    return jnp.where(jnp.arange(SEQS) == chosen, SEQ_LEN, drawn).astype(jnp.int32)


def level_of(key, shape, cuts, low, largest):
    def one(dim, parts):
        heights = jax.random.uniform(jax.random.fold_in(jax.random.fold_in(key, 6), dim), (parts,), jnp.float32, low / len(cuts), largest / len(cuts))
        return jnp.repeat(jnp.exp(heights), shape[dim] // parts).reshape((-1,) + (1,) * (len(shape) - dim - 1))

    factor_of = one(*cuts[0])
    for cut in cuts[1:]:
        factor_of = factor_of * one(*cut)
    return factor_of


def bell_draw(rng, shape, deviation, most, cuts=(), held_as=jnp.bfloat16):
    values = jax.random.normal(rng, shape, jnp.float32) * deviation
    if len(cuts) > 0:
        values = level_of(rng, shape, cuts, -0.22, 0.18) * values
    return jnp.clip(values, min=-most, max=most).astype(held_as)


def setup_inputs(seed: int = 0) -> dict:
    streams_of = jax.random.split(jax.random.key(seed), 14)
    return {
        "inputs": bell_draw(streams_of[0], (TOKENS, D), 1.0, 6.0, ((0, 16),)),
        "lengths": draw_lengths(jax.random.fold_in(streams_of[13], 71), 0),
        "gain_attn": jnp.clip(1.0 + 0.1 * jax.random.normal(streams_of[2], (D,), jnp.float32), 0.5, 1.5).astype(jnp.bfloat16),
        "w_query": bell_draw(streams_of[3], (D, HEADS * HEAD_DIM), D ** -0.5, 0.1875, ((1, 2),)),
        "w_key": bell_draw(streams_of[4], (D, HEADS * HEAD_DIM), D ** -0.5, 0.1875, ((1, 2),)),
        "w_value": bell_draw(streams_of[5], (D, HEADS * HEAD_DIM), D ** -0.5, 0.1875, ((1, 2),)),
        "w_gate_attn": bell_draw(streams_of[6], (D, HEADS * HEAD_DIM), D ** -0.5, 0.1875, ((1, 2),)),
        "w_out": bell_draw(streams_of[7], (HEADS * HEAD_DIM, D), (HEADS * HEAD_DIM // 2) ** -0.5, 0.25, ((0, 2),)),
        "gain_ffn": jnp.clip(1.0 + 0.1 * jax.random.normal(streams_of[8], (D,), jnp.float32), 0.5, 1.5).astype(jnp.bfloat16),
        "w_gate": bell_draw(streams_of[9], (D, FF), D ** -0.5, 0.1875, ((1, 2),)),
        "w_up": bell_draw(streams_of[10], (D, FF), D ** -0.5, 0.1875, ((1, 2),)),
        "w_down": bell_draw(streams_of[11], (FF, D), (FF // 2) ** -0.5, 0.15625, ((0, 2),)),
        "cotangent": bell_draw(streams_of[12], (TOKENS, D), 1.0, 6.0, ((0, 16),)),
    }


EPS = 1e-06
HIGHEST = lax.Precision.HIGHEST

@jax.custom_vjp
def low(v):
    return lax.optimization_barrier(v.astype(jnp.bfloat16)).astype(jnp.float32)

@jax.custom_vjp
def low_back(v):
    return v

def low_keep(v):
    return (low(v), None)

def low_pass(kept, grad):
    return (grad,)

def back_keep(v):
    return (v, None)

def back_low(kept, grad):
    return (low(grad),)
low.defvjp(low_keep, low_pass)
low_back.defvjp(back_keep, back_low)

def matmul(left, right):
    return jnp.dot(left, right, precision=HIGHEST)

def decay_tables(rates, block):
    kind = rates.dtype
    offset = jnp.arange(block).astype(kind)
    spread = offset[:, None] - offset[None, :]
    causal = (spread >= 0.0).astype(kind)
    within = jnp.exp(-rates[:, None, None] * (spread * causal)[None]) * causal[None]
    query_decay = jnp.exp(-rates[:, None] * (offset + 1.0)[None]).T[:, :, None]
    key_decay = jnp.exp(-rates[:, None] * (block - 1.0 - offset)[None]).T[:, :, None]
    block_decay = jnp.exp(-rates * block)[:, None, None]
    return (within, query_decay, key_decay, block_decay)

def seq_forward(params, residual_in, length):
    gain_one, w_query, w_key, w_value, w_gate_attn, w_out, gain_two, w_gate, w_up, w_down = params
    kind = residual_in.dtype
    seq_rows = residual_in.shape[0]
    positions = jnp.arange(seq_rows).astype(jnp.int32)
    live = (positions < length.astype(jnp.int32)).astype(kind)[:, None]
    scale_one = lax.rsqrt(lax.optimization_barrier(jnp.mean(residual_in * residual_in, axis=1, keepdims=True)) + EPS)
    hidden_one = low(residual_in * scale_one * gain_one)
    queries = low(jax.nn.softplus(low_back(matmul(hidden_one, w_query))))
    keys = low(jax.nn.softplus(low_back(matmul(hidden_one, w_key))) * live)
    values = low(low_back(matmul(hidden_one, w_value)))
    gate_attn = jax.nn.sigmoid(low_back(matmul(hidden_one, w_gate_attn)))
    head_ids = jnp.arange(HEADS).astype(kind)
    rates = jnp.power(jnp.asarray(2.0, kind), -8.0 * (head_ids + 1.0) / HEADS)
    within, query_decay, key_decay, block_decay = decay_tables(rates, BLOCK)
    blocks = seq_rows // BLOCK

    def attend(state, pieces):
        query_block, key_block, value_block = pieces
        scores = low_back(jnp.einsum('ihd,jhd->hij', query_block, key_block, precision=HIGHEST))
        weights = low(scores * within)
        local_part = jnp.einsum('hij,jhd->ihd', weights, value_block, precision=HIGHEST)
        carried = jnp.einsum('ihd,hde->ihe', query_block, state, precision=HIGHEST) * query_decay
        new_state = block_decay * state + jnp.einsum('jhd,jhe->hde', key_block * key_decay, value_block, precision=HIGHEST)
        return (new_state.astype(state.dtype), low_back(local_part + carried))

    def blocked(array):
        return array.reshape(blocks, BLOCK, HEADS, HEAD_DIM)
    start_state = jnp.zeros((HEADS, HEAD_DIM, HEAD_DIM), queries.dtype)
    final_state, block_outputs = lax.scan(jax.checkpoint(attend), start_state, (blocked(queries), blocked(keys), blocked(values)))
    attended = block_outputs.reshape(seq_rows, HEADS, HEAD_DIM)
    scale_out = lax.rsqrt(lax.optimization_barrier(jnp.mean(attended * attended, axis=2, keepdims=True)) + EPS)
    normed_out = attended * scale_out
    mixed = low((normed_out * gate_attn.reshape(seq_rows, HEADS, HEAD_DIM)).reshape(seq_rows, HEADS * HEAD_DIM))
    attn_branch = low_back(matmul(mixed, w_out))
    residual_mid = residual_in + live * attn_branch
    scale_two = lax.rsqrt(lax.optimization_barrier(jnp.mean(residual_mid * residual_mid, axis=1, keepdims=True)) + EPS)
    hidden_two = low(residual_mid * scale_two * gain_two)
    gate_pre = low_back(matmul(hidden_two, w_gate))
    up_pre = low_back(matmul(hidden_two, w_up))
    glu = low(jax.nn.silu(gate_pre) * up_pre)
    ffn_branch = low_back(matmul(glu, w_down))
    return residual_mid + live * ffn_branch

def forward(params, whole_input, lengths):
    sequences = whole_input.reshape(SEQS, SEQ_LEN, D)
    checked = jax.checkpoint(seq_forward)

    def one_seq(pieces):
        return checked(params, pieces[0], pieces[1])
    outputs = lax.map(one_seq, (sequences, lengths.astype(jnp.int32)))
    return outputs.reshape(TOKENS, D)

def reference(inputs, lengths, gain_attn, w_query, w_key, w_value, w_gate_attn, w_out, gain_ffn, w_gate, w_up, w_down, cotangent):
    params = (gain_attn.astype(jnp.float32), w_query.astype(jnp.float32), w_key.astype(jnp.float32), w_value.astype(jnp.float32), w_gate_attn.astype(jnp.float32), w_out.astype(jnp.float32), gain_ffn.astype(jnp.float32), w_gate.astype(jnp.float32), w_up.astype(jnp.float32), w_down.astype(jnp.float32))
    whole_input = inputs.astype(jnp.float32)

    def run(weights, entries):
        return forward(weights, entries, lengths)
    outputs, pull = jax.vjp(run, params, whole_input)
    grads, entry_grad = pull(cotangent.astype(jnp.float32))
    return (outputs.astype(jnp.bfloat16), entry_grad.astype(jnp.bfloat16), grads[0], grads[1], grads[2], grads[3], grads[4], grads[5], grads[6], grads[7], grads[8], grads[9])
```

```python
import functools

import jax
import jax.numpy as jnp
from jax import lax
from jax.experimental import pallas as pl
from jax.experimental.pallas import tpu as pltpu
from jax.sharding import PartitionSpec as P

HEADS = 16
HEAD_DIM = 64
BLOCK = 512
EPS = 1e-06
HIGHEST = lax.Precision.HIGHEST
F32 = jnp.float32
BF16 = jnp.bfloat16


def matmul(left, right):
    return jnp.dot(left, right, preferred_element_type=F32)


def times_transpose(left, right):
    return lax.dot_general(left, right, (((1,), (1,)), ((), ())), preferred_element_type=F32)


def row_mean(array):
    return jnp.mean(array, axis=1, keepdims=True)


MIB = 2**20
TILE = 256
CHUNK = 256
PAIR = 2 * HEAD_DIM


def whole(array):
    return pl.BlockSpec(array.shape, lambda *_: (0,) * array.ndim, pipeline_mode=pl.Buffered(1))


def row_tile(columns, rows=TILE):
    return pl.BlockSpec((rows, columns), lambda step: (step, 0))


def call(body, grid, ins, in_specs, outs, out_specs, flops, scratch=(), limit=56):
    return pl.pallas_call(
        body,
        grid=grid,
        in_specs=in_specs,
        out_specs=out_specs,
        out_shape=outs,
        scratch_shapes=scratch,
        cost_estimate=pl.CostEstimate(flops=int(flops), bytes_accessed=8 * MIB, transcendentals=0),
        compiler_params=pltpu.CompilerParams(vmem_limit_bytes=limit * MIB),
    )(*ins)


def shaped(rows, columns, kind=BF16):
    return jax.ShapeDtypeStruct((rows, columns), kind)


def norm_kernel(inputs_ref, gain_ref, hidden_ref):
    wide = inputs_ref[...].astype(F32)
    scale = lax.rsqrt(row_mean(wide * wide) + EPS)
    hidden_ref[...] = (wide * scale * gain_ref[...].astype(F32)).astype(BF16)


def first_norm(inputs, gain):
    rows, width = inputs.shape
    return call(
        norm_kernel,
        (rows // TILE,),
        (inputs, gain),
        [row_tile(width), whole(gain)],
        shaped(rows, width),
        row_tile(width),
        rows * width * 8,
    )


def project_kernel(hidden_ref, live_ref, wq_ref, wk_ref, wv_ref, wg_ref, q_ref, sq_ref, k_ref, sk_ref, v_ref, gate_ref):
    hidden = hidden_ref[...]
    live = live_ref[...]

    def activate(value):
        small = jnp.exp(-jnp.abs(value))
        share = 1.0 / (1.0 + small)
        return jnp.maximum(value, 0.0) + jnp.log1p(small), jnp.where(value >= 0.0, share, small * share)

    positive, slope = activate(matmul(hidden, wq_ref[...]))
    q_ref[...] = positive.astype(BF16)
    sq_ref[...] = slope.astype(BF16)
    positive, slope = activate(matmul(hidden, wk_ref[...]))
    k_ref[...] = (positive * live).astype(BF16)
    sk_ref[...] = (slope * live).astype(BF16)
    v_ref[...] = matmul(hidden, wv_ref[...]).astype(BF16)
    gate_ref[...] = jax.nn.sigmoid(matmul(hidden, wg_ref[...]))


def project(hidden, live, weights):
    rows, width = hidden.shape
    columns = weights[0].shape[1]
    narrow = shaped(rows, columns)
    return call(
        project_kernel,
        (rows // TILE,),
        (hidden, live, *weights),
        [row_tile(width), row_tile(1)] + [whole(w) for w in weights],
        [narrow] * 5 + [shaped(rows, columns, F32)],
        [row_tile(columns)] * 6,
        8 * rows * width * columns,
    )


def head_lanes():
    return lax.broadcasted_iota(jnp.int32, (1, PAIR), 1) < HEAD_DIM


def same_head():
    rows = lax.broadcasted_iota(jnp.int32, (PAIR, PAIR), 0) < HEAD_DIM
    columns = lax.broadcasted_iota(jnp.int32, (PAIR, PAIR), 1) < HEAD_DIM
    return rows == columns


def head_mean(array, ones):
    high = array.astype(BF16)
    low = (array - high.astype(F32)).astype(BF16)
    return (matmul(high, ones) + matmul(low, ones)) * (1.0 / HEAD_DIM)


def decays(rate_ref):
    pair = pl.program_id(0)
    rates = (rate_ref[2 * pair], rate_ref[2 * pair + 1])
    lane_rate = jnp.where(head_lanes(), rates[0], rates[1])
    place = lax.broadcasted_iota(jnp.int32, (CHUNK, 1), 0).astype(F32)
    query_decay = jnp.exp(-lane_rate * (place + 1.0))
    key_decay = jnp.exp(-lane_rate * (CHUNK - 1.0 - place))
    chunk_decay = jnp.exp(-lane_rate * CHUNK)
    return rates, query_decay, key_decay, chunk_decay


def within_table(rate, flipped=False):
    rows = lax.broadcasted_iota(jnp.int32, (CHUNK, CHUNK), 0)
    columns = lax.broadcasted_iota(jnp.int32, (CHUNK, CHUNK), 1)
    spread = columns - rows if flipped else rows - columns
    kept = spread >= 0
    return jnp.where(kept, jnp.exp(-rate * jnp.where(kept, spread, 0).astype(F32)), 0.0)


def attend_kernel(rate_ref, q_ref, k_ref, v_ref, gate_ref, attended_ref, mixed_ref):
    rates, query_decay, key_decay, chunk_decay = decays(rate_ref)
    first = head_lanes()
    same = same_head()
    ones = jnp.where(same, 1.0, 0.0).astype(BF16)
    tables = [within_table(rate) for rate in rates]
    masks = [jnp.where(first, 1.0, 0.0).astype(BF16), jnp.where(first, 0.0, 1.0).astype(BF16)]
    state = jnp.zeros((PAIR, PAIR), F32)
    for index in range(q_ref.shape[0] // CHUNK):
        rows = pl.ds(index * CHUNK, CHUNK)
        q, k, v = q_ref[rows, :], k_ref[rows, :], v_ref[rows, :]
        attended = matmul(q, state.astype(BF16)) * query_decay
        for mask, table in zip(masks, tables):
            weights = (times_transpose(q * mask, k) * table).astype(BF16)
            attended = attended + matmul(weights, v * mask)
        keys = (k.astype(F32) * key_decay).T.astype(BF16)
        state = chunk_decay * state + jnp.where(same, matmul(keys, v), 0.0)
        scale = lax.rsqrt(head_mean(attended * attended, ones) + EPS)
        attended_ref[rows, :] = attended
        mixed_ref[rows, :] = (attended * scale * gate_ref[rows, :]).astype(BF16)


def pair_spec(rows):
    return pl.BlockSpec((rows, PAIR), lambda pair: (0, pair))


def attend(q, k, v, gate, rates):
    rows, columns = q.shape
    return call(
        attend_kernel,
        (columns // PAIR,),
        (rates, q, k, v, gate),
        [pl.BlockSpec(memory_space=pltpu.SMEM)] + [pair_spec(rows)] * 4,
        [shaped(rows, columns, F32), shaped(rows, columns)],
        [pair_spec(rows)] * 2,
        12 * rows * columns * CHUNK,
    )


def attend_back_kernel(
    rate_ref, q_ref, sq_ref, k_ref, sk_ref, v_ref, gate_ref, attended_ref, grad_ref, wo_ref,
    dq_ref, dk_ref, dv_ref, dg_ref, out_grad, states,
):
    rates, query_decay, key_decay, chunk_decay = decays(rate_ref)
    first = head_lanes()
    same = same_head()
    ones = jnp.where(same, 1.0, 0.0).astype(BF16)
    tables = [within_table(rate) for rate in rates]
    flipped = [within_table(rate, True) for rate in rates]
    masks = [jnp.where(first, 1.0, 0.0).astype(BF16), jnp.where(first, 0.0, 1.0).astype(BF16)]
    chunks = q_ref.shape[0] // CHUNK
    state = jnp.zeros((PAIR, PAIR), F32)
    for index in range(chunks):
        rows = pl.ds(index * CHUNK, CHUNK)
        mixed_grad = times_transpose(grad_ref[rows, :], wo_ref[...])
        attended, gate = attended_ref[rows, :], gate_ref[rows, :]
        scale = lax.rsqrt(head_mean(attended * attended, ones) + EPS)
        normed = attended * scale
        dg_ref[rows, :] = (mixed_grad * normed * gate * (1.0 - gate)).astype(BF16)
        normed_grad = mixed_grad * gate
        out_grad[rows, :] = (scale * (normed_grad - normed * head_mean(normed_grad * normed, ones))).astype(BF16)
        states[index] = state.astype(BF16)
        if index < chunks - 1:
            keys = (k_ref[rows, :].astype(F32) * key_decay).T.astype(BF16)
            state = chunk_decay * state + jnp.where(same, matmul(keys, v_ref[rows, :]), 0.0)
    carry = jnp.zeros((PAIR, PAIR), F32)
    for index in reversed(range(chunks)):
        rows = pl.ds(index * CHUNK, CHUNK)
        q, k, v, grad = q_ref[rows, :], k_ref[rows, :], v_ref[rows, :], out_grad[rows, :]
        narrow = carry.astype(BF16)
        dq = times_transpose(grad, states[index]) * query_decay
        dk = times_transpose(v, narrow) * key_decay
        dv = matmul(k, narrow) * key_decay
        for mask, table, turned in zip(masks, tables, flipped):
            q_one, grad_one = q * mask, grad * mask
            weights = (times_transpose(k, q_one) * turned).astype(BF16)
            dv = dv + matmul(weights, grad_one)
            dq = dq + matmul((times_transpose(grad_one, v) * table).astype(BF16), k * mask)
            dk = dk + matmul((times_transpose(v, grad_one) * turned).astype(BF16), q_one)
        dq_ref[rows, :] = (dq * sq_ref[rows, :].astype(F32)).astype(BF16)
        dk_ref[rows, :] = (dk * sk_ref[rows, :].astype(F32)).astype(BF16)
        dv_ref[rows, :] = dv.astype(BF16)
        if index > 0:
            turned_q = q.astype(F32).T.astype(BF16)
            decayed = (grad.astype(F32) * query_decay).astype(BF16)
            carry = chunk_decay * carry + jnp.where(same, matmul(turned_q, decayed), 0.0)


def attend_back(half, out_grad, w_out):
    q, sq, k, sk, v, gate, attended, rates = half
    rows, columns = q.shape
    width = out_grad.shape[1]
    return call(
        attend_back_kernel,
        (columns // PAIR,),
        (rates, q, sq, k, sk, v, gate, attended, out_grad, w_out),
        [pl.BlockSpec(memory_space=pltpu.SMEM)]
        + [pair_spec(rows)] * 7
        + [whole(out_grad), pl.BlockSpec((PAIR, width), lambda pair: (pair, 0))],
        [shaped(rows, columns)] * 4,
        [pair_spec(rows)] * 4,
        2 * rows * columns * width + 30 * rows * columns * CHUNK,
        scratch=[pltpu.VMEM((rows, PAIR), BF16), pltpu.VMEM((rows // CHUNK, PAIR, PAIR), BF16)],
    )


def glu_parts(hidden, out_grad, wg_ref, wu_ref, wd_ref, columns):
    gate_pre = matmul(hidden, wg_ref[:, columns])
    up_pre = matmul(hidden, wu_ref[:, columns])
    glu_grad = times_transpose(out_grad, wd_ref[columns, :])
    logistic = jax.nn.sigmoid(gate_pre)
    act = gate_pre * logistic
    glu = (act * up_pre).astype(BF16)
    up_grad = (glu_grad * act).astype(BF16)
    gate_grad = (glu_grad * up_pre * (logistic * (1.0 + gate_pre * (1.0 - logistic)))).astype(BF16)
    return glu, gate_grad, up_grad


def unit_slices(units):
    step = 512
    return [slice(low, min(low + step, units)) for low in range(0, units, step)]


def middle_kernel(
    inputs_ref, live_ref, dy_ref, mixed_a_ref, mixed_b_ref, wo_a_ref, wo_b_ref, gain_ref, wg_ref, wu_ref, wd_ref,
    residual_ref, hidden_ref, glu_ref, gate_grad_ref, up_grad_ref, branch_ref, back_ref,
):
    live = live_ref[...]
    branch = matmul(mixed_a_ref[...], wo_a_ref[...]) + matmul(mixed_b_ref[...], wo_b_ref[...])
    residual = inputs_ref[...].astype(F32) + live * branch
    residual_ref[...] = residual
    scale = lax.rsqrt(row_mean(residual * residual) + EPS)
    hidden = (residual * scale * gain_ref[...].astype(F32)).astype(BF16)
    hidden_ref[...] = hidden
    out_grad = (live * dy_ref[...].astype(F32)).astype(BF16)
    units = wg_ref.shape[1]
    for columns in unit_slices(units):
        glu, gate_grad, up_grad = glu_parts(hidden, out_grad, wg_ref, wu_ref, wd_ref, columns)
        glu_ref[:, columns] = glu
        gate_grad_ref[:, columns] = gate_grad
        up_grad_ref[:, columns] = up_grad
    branch_ref[...] = matmul(glu_ref[...], wd_ref[...])
    back_ref[...] = times_transpose(gate_grad_ref[...], wg_ref[...]) + times_transpose(up_grad_ref[...], wu_ref[...])


def middle(inputs, live, dy, mixed, outs, gain, glus):
    rows, width = inputs.shape
    heads = mixed[0].shape[1]
    units = glus[0].shape[1]
    return call(
        middle_kernel,
        (rows // TILE,),
        (inputs, live, dy, *mixed, *outs, gain, *glus),
        [row_tile(width), row_tile(1), row_tile(width), row_tile(heads), row_tile(heads)]
        + [whole(w) for w in (*outs, gain, *glus)],
        [shaped(rows, width, F32), shaped(rows, width)]
        + [shaped(rows, units)] * 3
        + [shaped(rows, width, F32)] * 2,
        [row_tile(width)] * 2 + [row_tile(units)] * 3 + [row_tile(width)] * 2,
        2 * rows * width * (2 * heads + 6 * units),
    )


def norm_back(grad, normed, scale):
    return scale * (grad - normed * row_mean(grad * normed))


def middle_back_kernel(
    residual_ref, hidden_ref, live_ref, dy_ref, branch_ref, back_ref, gain_ref, wg_ref, wu_ref, wd_ref,
    result_ref, mid_ref, grad_ref, gain_grad_ref, glu_buf, gate_buf, up_buf,
):
    live = live_ref[...]
    dy = dy_ref[...].astype(F32)
    hidden = hidden_ref[...]
    out_grad = (live * dy).astype(BF16)
    for columns in unit_slices(wg_ref.shape[1]):
        glu_buf[:, columns], gate_buf[:, columns], up_buf[:, columns] = glu_parts(
            hidden, out_grad, wg_ref, wu_ref, wd_ref, columns
        )
    residual = residual_ref[...]
    branch = branch_ref[...] + matmul(glu_buf[...], wd_ref[...])
    result_ref[...] = (residual + live * branch).astype(BF16)
    back = back_ref[...] + times_transpose(gate_buf[...], wg_ref[...]) + times_transpose(up_buf[...], wu_ref[...])
    scale = lax.rsqrt(row_mean(residual * residual) + EPS)
    normed = residual * scale

    @pl.when(pl.program_id(0) == 0)
    def _():
        gain_grad_ref[...] = jnp.zeros_like(gain_grad_ref)

    gain_grad_ref[...] += jnp.sum(back * normed, axis=0, keepdims=True)
    mid = dy + norm_back(back * gain_ref[...].astype(F32), normed, scale)
    mid_ref[...] = mid
    grad_ref[...] = (live * mid).astype(BF16)


def middle_back(residual, hidden, live, dy, branch, back, gain, glus):
    rows, width = hidden.shape
    units = glus[0].shape[1]
    return call(
        middle_back_kernel,
        (rows // TILE,),
        (residual, hidden, live, dy, branch, back, gain, *glus),
        [row_tile(width), row_tile(width), row_tile(1)]
        + [row_tile(width)] * 3
        + [whole(w) for w in (gain, *glus)],
        [shaped(rows, width), shaped(rows, width, F32), shaped(rows, width), shaped(1, width, F32)],
        [row_tile(width)] * 3 + [pl.BlockSpec((1, width), lambda step: (0, 0))],
        2 * rows * width * 6 * units,
        scratch=[pltpu.VMEM((TILE, units), BF16)] * 3,
    )


def first_back_kernel(inputs_ref, mid_ref, gain_ref, *refs):
    grads, weights, (result_ref, gain_grad_ref) = refs[:8], refs[8:16], refs[16:]
    back = times_transpose(grads[0][...], weights[0][...])
    for grad, weight in zip(grads[1:], weights[1:]):
        back = back + times_transpose(grad[...], weight[...])
    wide = inputs_ref[...].astype(F32)
    scale = lax.rsqrt(row_mean(wide * wide) + EPS)
    normed = wide * scale

    @pl.when(pl.program_id(0) == 0)
    def _():
        gain_grad_ref[...] = jnp.zeros_like(gain_grad_ref)

    gain_grad_ref[...] += jnp.sum(back * normed, axis=0, keepdims=True)
    result_ref[...] = (mid_ref[...] + norm_back(back * gain_ref[...].astype(F32), normed, scale)).astype(BF16)


def first_back(inputs, mid, gain, grads, weights):
    rows, width = inputs.shape
    columns = weights[0].shape[1]
    return call(
        first_back_kernel,
        (rows // TILE,),
        (inputs, mid, gain, *grads, *weights),
        [row_tile(width), row_tile(width), whole(gain)]
        + [row_tile(columns)] * 8
        + [whole(w) for w in weights],
        [shaped(rows, width), shaped(1, width, F32)],
        [row_tile(width), pl.BlockSpec((1, width), lambda step: (0, 0))],
        2 * rows * width * columns * 8,
    )


def product_kernel(left_ref, right_ref, *refs):
    total = matmul(left_ref[...], right_ref[...])
    if len(refs) == 2:
        total = total + refs[0][...]
    refs[-1][...] = total


def product(left, right, first, count, came=None, came_first=0):
    depth, columns = right.shape
    tile = min(TILE, count)
    ins = [left, right]
    specs = [pl.BlockSpec((tile, depth), lambda step: (first // tile + step, 0)), whole(right)]
    if came is not None:
        ins.append(came)
        specs.append(pl.BlockSpec((tile, columns), lambda step: (came_first // tile + step, 0)))
    return call(
        product_kernel,
        (count // tile,),
        tuple(ins),
        specs,
        shaped(count, columns, F32),
        row_tile(columns, tile),
        2 * count * depth * columns,
    )


CORE, ACROSS_X, NEAR_Z, FAR_Z = 1, 2, 4, 8


def swap_dp(array, bit, size):
    return lax.ppermute(array, "dp", [(place, place ^ bit) for place in range(size)])


def swap_tensor(array):
    return lax.ppermute(array, "tensor", [(0, 1), (1, 0)])


def place_kernel(place_ref, *refs):
    step = pl.program_id(0)
    for index in range(8):

        @pl.when(step == index)
        def _(index=index):
            refs[8][...] = refs[index][...].astype(BF16)


def cast_kernel(wide_ref, out_ref):
    out_ref[...] = wide_ref[...].astype(BF16)


def cast_weight(wide):
    rows, columns = wide.shape
    spec = pl.BlockSpec((rows // 8, columns), lambda row: (row, 0))
    return pl.pallas_call(
        cast_kernel, grid=(8,), out_shape=jax.ShapeDtypeStruct(wide.shape, BF16), in_specs=[spec], out_specs=spec
    )(wide)


def gather_other(weights, place, dp_size):
    if dp_size != 16:
        return [cast_weight(swap_tensor(weight.astype(F32))) for weight in weights]
    count = len(weights)
    rows, columns = weights[0].shape
    part = rows // 8

    def piece(index):
        return jnp.concatenate(
            [lax.dynamic_slice_in_dim(w, index * part, part, 0).astype(F32) for w in weights], axis=0
        )

    own = swap_tensor(piece(place))
    diagonal = swap_tensor(piece(place ^ 6))
    from_x = swap_dp(own, ACROSS_X, 16)
    from_z = swap_dp(own, NEAR_Z, 16)
    even = {0: own, 2: from_x, 4: from_z, 6: diagonal}
    odd = {index + 1: swap_dp(array, CORE, 16) for index, array in even.items()}
    pieces = {**even, **odd}
    placed = []
    for which in range(count):
        placed.append(
            pl.pallas_call(
                place_kernel,
                out_shape=jax.ShapeDtypeStruct((rows, columns), BF16),
                grid_spec=pltpu.PrefetchScalarGridSpec(
                    num_scalar_prefetch=1,
                    grid=(8,),
                    in_specs=[pl.BlockSpec((part, columns), lambda step, ref, which=which: (which, 0))] * 8,
                    out_specs=pl.BlockSpec((part, columns), lambda step, ref: (ref[0] ^ step, 0)),
                ),
                compiler_params=pltpu.CompilerParams(vmem_limit_bytes=40 * 2**20),
            )(place.reshape(1), *[pieces[index] for index in range(8)])
        )
    return placed


def relative_rows(array, dp_place, order, dp_size):
    if dp_size != 16:
        return array
    blocks = array.reshape(2, 2, 2, 2, array.shape[0] // 16, array.shape[1])
    for axis, bit in enumerate((FAR_Z, NEAR_Z, ACROSS_X, CORE)):
        blocks = jnp.where((dp_place & bit) > 0, jnp.flip(blocks, axis), blocks)
    axes = {FAR_Z: 0, NEAR_Z: 1, ACROSS_X: 2, CORE: 3}
    return blocks.transpose([axes[bit] for bit in order] + [4, 5]).reshape(array.shape)


def scatter_product(left, right, order, dp_size):
    if dp_size != 16:
        return lax.psum_scatter(matmul(left, right), "dp", scatter_dimension=0, tiled=True)
    size = left.shape[0]
    half = size // 4
    came = swap_dp(product(left, right, 2 * half, 2 * half), order[0], 16)
    came_next = swap_dp(product(left, right, half, half, came, half), order[1], 16)
    kept = product(left, right, 0, half, came, 0)
    for bit in order[2:]:
        half = kept.shape[0] // 2
        send = kept[half:] + came_next[half:]
        kept = kept[:half] + came_next[:half]
        came_next = swap_dp(send, bit, 16)
    return kept + came_next


def scatter_vector(vector, dp_place, dp_size):
    if dp_size != 16:
        return lax.psum_scatter(vector, "dp", scatter_dimension=0, tiled=True)
    order = (CORE, ACROSS_X, NEAR_Z, FAR_Z)
    kept = relative_rows(vector, dp_place, order, dp_size)
    for bit in order:
        half = kept.shape[0] // 2
        kept = kept[:half] + swap_dp(kept[half:], bit, 16)
    return kept


def shards_here(
    dp_size, inputs, lengths, gain_attn, w_query, w_key, w_value, w_gate_attn, w_out, gain_ffn, w_gate, w_up, w_down, cotangent
):
    seq_rows = inputs.shape[0]
    local_heads = w_query.shape[1] // HEAD_DIM
    side = lax.axis_index("tensor")
    dp_place = lax.axis_index("dp")
    place = dp_place % 8
    others_qk = gather_other([w_query, w_key], place, dp_size)
    others_vg = gather_other([w_value, w_gate_attn], place, dp_size)
    others_out = gather_other([w_out], place, dp_size)
    others_gu = gather_other([w_gate, w_up], place, dp_size)
    others_down = gather_other([w_down], place, dp_size)
    projections = ((w_query, w_key, w_value, w_gate_attn), tuple(others_qk) + tuple(others_vg))
    outs = (w_out, others_out[0])
    glus = ((w_gate, w_up, w_down), (others_gu[0], others_gu[1], others_down[0]))
    head_ids = jnp.arange(local_heads)
    rates = tuple(
        jnp.exp2(-8.0 * ((which * local_heads + head_ids).astype(F32) + 1.0) / HEADS)
        for which in (side, 1 - side)
    )
    positions = jnp.arange(seq_rows, dtype=jnp.int32)
    live = (positions < lengths[0]).astype(F32)[:, None]
    gain_one = gain_attn.reshape(1, -1)
    gain_two = gain_ffn.reshape(1, -1)
    ffn_out_grad = (live * cotangent.astype(F32)).astype(BF16)

    hidden_one = first_norm(inputs, gain_one)
    halves = []
    mixed = []
    for half in range(2):
        parts = project(hidden_one, live, projections[half])
        q, sq, k, sk, v, gate = parts
        attended, mixed_half = attend(q, k, v, gate, rates[half])
        halves.append((*parts, attended, rates[half]))
        mixed.append(mixed_half)
    residual, hidden_two, glu, gate_grad, up_grad, branch, back = middle(
        inputs, live, cotangent, mixed, outs, gain_two, glus[0]
    )
    order = (CORE, ACROSS_X, NEAR_Z, FAR_Z)
    order_z = (CORE, NEAR_Z, FAR_Z, ACROSS_X)
    ffn_out_grad_t = relative_rows(ffn_out_grad.T, dp_place, order_z, dp_size)
    grad_down = scatter_product(ffn_out_grad_t, glu, order_z, dp_size)
    hidden_two_t = relative_rows(hidden_two.T, dp_place, order, dp_size)
    grad_gate = scatter_product(hidden_two_t, gate_grad, order, dp_size)
    grad_up = scatter_product(hidden_two_t, up_grad, order, dp_size)
    result, mid_grad, attn_out_grad, gain_two_grad = middle_back(
        residual, hidden_two, live, cotangent, branch, back, gain_two, glus[1]
    )
    attn_out_grad_t = relative_rows(attn_out_grad.T, dp_place, order, dp_size)
    hidden_one_t = relative_rows(hidden_one.T, dp_place, order, dp_size)
    own = attend_back(halves[0], attn_out_grad, outs[0])
    grad_out = scatter_product(attn_out_grad_t, mixed[0], order, dp_size)
    grad_query, grad_key, grad_value, grad_gate_attn = [
        scatter_product(hidden_one_t, grad, order, dp_size) for grad in own
    ]
    other = attend_back(halves[1], attn_out_grad, outs[1])
    input_grad, gain_one_grad = first_back(
        inputs, mid_grad, gain_one, (*own, *other), (*projections[0], *projections[1])
    )
    gains = scatter_vector(
        jnp.concatenate([gain_one_grad, gain_two_grad], axis=0).T, dp_place, dp_size
    )
    return (
        result,
        input_grad,
        gains[:, 0],
        grad_query,
        grad_key,
        grad_value,
        grad_gate_attn,
        grad_out.T,
        gains[:, 1],
        grad_gate,
        grad_up,
        grad_down.T,
    )


def solution(mesh):
    placed = (
        P("dp", None),
        P("dp"),
        P(),
        P(None, "tensor"),
        P(None, "tensor"),
        P(None, "tensor"),
        P(None, "tensor"),
        P("tensor", None),
        P(),
        P(None, "tensor"),
        P(None, "tensor"),
        P("tensor", None),
        P("dp", None),
    )
    return jax.shard_map(
        functools.partial(shards_here, mesh.shape["dp"]),
        mesh=mesh,
        in_specs=placed,
        out_specs=(
            P("dp", None),
            P("dp", None),
            P("dp"),
            P("dp", "tensor"),
            P("dp", "tensor"),
            P("dp", "tensor"),
            P("dp", "tensor"),
            P("tensor", "dp"),
            P("dp"),
            P("dp", "tensor"),
            P("dp", "tensor"),
            P("tensor", "dp"),
        ),
        check_vma=False,
    )
```

```python
import functools

import jax
import jax.numpy as jnp
from jax import lax
from jax.experimental import pallas as pl
from jax.experimental.pallas import tpu as pltpu
from jax.sharding import PartitionSpec as P

HEADS = 16
HEAD_DIM = 64
BLOCK = 512
EPS = 1e-06
HIGHEST = lax.Precision.HIGHEST
F32 = jnp.float32
BF16 = jnp.bfloat16


def matmul(left, right):
    return jnp.dot(left, right, preferred_element_type=F32)


def times_transpose(left, right):
    return lax.dot_general(left, right, (((1,), (1,)), ((), ())), preferred_element_type=F32)


def row_mean(array):
    return jnp.mean(array, axis=1, keepdims=True)


MIB = 2**20
COST = 1000
TILE = 256
CHUNK = 256
PAIR = 2 * HEAD_DIM


def whole(array):
    return pl.BlockSpec(array.shape, lambda *_: (0,) * array.ndim, pipeline_mode=pl.Buffered(1))


def row_tile(columns, rows=TILE):
    return pl.BlockSpec((rows, columns), lambda step: (step, 0))


def call(body, grid, ins, in_specs, outs, out_specs, flops, scratch=(), limit=34):
    return pl.pallas_call(
        body,
        grid=grid,
        in_specs=in_specs,
        out_specs=out_specs,
        out_shape=outs,
        scratch_shapes=scratch,
        cost_estimate=pl.CostEstimate(flops=int(flops) // COST, bytes_accessed=1024, transcendentals=0),
        compiler_params=pltpu.CompilerParams(vmem_limit_bytes=limit * MIB),
    )(*ins)


def shaped(rows, columns, kind=BF16):
    return jax.ShapeDtypeStruct((rows, columns), kind)


def norm_kernel(inputs_ref, gain_ref, hidden_ref):
    wide = inputs_ref[...].astype(F32)
    scale = lax.rsqrt(row_mean(wide * wide) + EPS)
    hidden_ref[...] = (wide * scale * gain_ref[...].astype(F32)).astype(BF16)


def first_norm(inputs, gain):
    rows, width = inputs.shape
    return call(
        norm_kernel,
        (rows // TILE,),
        (inputs, gain),
        [row_tile(width), whole(gain)],
        shaped(rows, width),
        row_tile(width),
        rows * width * 8,
    )


def project_kernel(hidden_ref, live_ref, wq_ref, wk_ref, wv_ref, wg_ref, q_ref, sq_ref, k_ref, sk_ref, v_ref, gate_ref):
    hidden = hidden_ref[...]
    live = live_ref[...]

    def activate(value):
        small = jnp.exp(-jnp.abs(value))
        share = 1.0 / (1.0 + small)
        return jnp.maximum(value, 0.0) + jnp.log1p(small), jnp.where(value >= 0.0, share, small * share)

    positive, slope = activate(matmul(hidden, wq_ref[...]))
    q_ref[...] = positive.astype(BF16)
    sq_ref[...] = slope.astype(BF16)
    positive, slope = activate(matmul(hidden, wk_ref[...]))
    k_ref[...] = (positive * live).astype(BF16)
    sk_ref[...] = (slope * live).astype(BF16)
    v_ref[...] = matmul(hidden, wv_ref[...]).astype(BF16)
    gate_ref[...] = jax.nn.sigmoid(matmul(hidden, wg_ref[...]))


def project(hidden, live, weights):
    rows, width = hidden.shape
    columns = weights[0].shape[1]
    narrow = shaped(rows, columns)
    return call(
        project_kernel,
        (rows // TILE,),
        (hidden, live, *weights),
        [row_tile(width), row_tile(1)] + [whole(w) for w in weights],
        [narrow] * 5 + [shaped(rows, columns, F32)],
        [row_tile(columns)] * 6,
        8 * rows * width * columns,
    )


def head_lanes():
    return lax.broadcasted_iota(jnp.int32, (1, PAIR), 1) < HEAD_DIM


def same_head():
    rows = lax.broadcasted_iota(jnp.int32, (PAIR, PAIR), 0) < HEAD_DIM
    columns = lax.broadcasted_iota(jnp.int32, (PAIR, PAIR), 1) < HEAD_DIM
    return rows == columns


def head_mean(array, ones):
    high = array.astype(BF16)
    low = (array - high.astype(F32)).astype(BF16)
    return (matmul(high, ones) + matmul(low, ones)) * (1.0 / HEAD_DIM)


def decays(rate_ref):
    pair = pl.program_id(0)
    rates = (rate_ref[2 * pair], rate_ref[2 * pair + 1])
    lane_rate = jnp.where(head_lanes(), rates[0], rates[1])
    place = lax.broadcasted_iota(jnp.int32, (CHUNK, 1), 0).astype(F32)
    query_decay = jnp.exp(-lane_rate * (place + 1.0))
    key_decay = jnp.exp(-lane_rate * (CHUNK - 1.0 - place))
    chunk_decay = jnp.exp(-lane_rate * CHUNK)
    return rates, query_decay, key_decay, chunk_decay


def within_table(rate, flipped=False):
    rows = lax.broadcasted_iota(jnp.int32, (CHUNK, CHUNK), 0)
    columns = lax.broadcasted_iota(jnp.int32, (CHUNK, CHUNK), 1)
    spread = columns - rows if flipped else rows - columns
    kept = spread >= 0
    return jnp.where(kept, jnp.exp(-rate * jnp.where(kept, spread, 0).astype(F32)), 0.0)


def attend_kernel(rate_ref, q_ref, k_ref, v_ref, gate_ref, attended_ref, mixed_ref):
    rates, query_decay, key_decay, chunk_decay = decays(rate_ref)
    first = head_lanes()
    same = same_head()
    ones = jnp.where(same, 1.0, 0.0).astype(BF16)
    tables = [within_table(rate) for rate in rates]
    masks = [jnp.where(first, 1.0, 0.0).astype(BF16), jnp.where(first, 0.0, 1.0).astype(BF16)]
    state = jnp.zeros((PAIR, PAIR), F32)
    for index in range(q_ref.shape[0] // CHUNK):
        rows = pl.ds(index * CHUNK, CHUNK)
        q, k, v = q_ref[rows, :], k_ref[rows, :], v_ref[rows, :]
        attended = matmul(q, state.astype(BF16)) * query_decay
        for mask, table in zip(masks, tables):
            weights = (times_transpose(q * mask, k) * table).astype(BF16)
            attended = attended + matmul(weights, v * mask)
        keys = (k.astype(F32) * key_decay).T.astype(BF16)
        state = chunk_decay * state + jnp.where(same, matmul(keys, v), 0.0)
        scale = lax.rsqrt(head_mean(attended * attended, ones) + EPS)
        attended_ref[rows, :] = attended
        mixed_ref[rows, :] = (attended * scale * gate_ref[rows, :]).astype(BF16)


def pair_spec(rows):
    return pl.BlockSpec((rows, PAIR), lambda pair: (0, pair))


def attend(q, k, v, gate, rates):
    rows, columns = q.shape
    return call(
        attend_kernel,
        (columns // PAIR,),
        (rates, q, k, v, gate),
        [pl.BlockSpec(memory_space=pltpu.SMEM)] + [pair_spec(rows)] * 4,
        [shaped(rows, columns, F32), shaped(rows, columns)],
        [pair_spec(rows)] * 2,
        12 * rows * columns * CHUNK,
    )


def open_back_kernel(gate_ref, attended_ref, grad_ref, wo_ref, out_grad_ref, dg_ref):
    ones = jnp.where(same_head(), 1.0, 0.0).astype(BF16)
    wide = times_transpose(grad_ref[...], wo_ref[...])
    for low in range(0, wide.shape[1], PAIR):
        lanes = slice(low, low + PAIR)
        mixed_grad, attended, gate = wide[:, lanes], attended_ref[:, lanes], gate_ref[:, lanes]
        scale = lax.rsqrt(head_mean(attended * attended, ones) + EPS)
        normed = attended * scale
        dg_ref[:, lanes] = (mixed_grad * normed * gate * (1.0 - gate)).astype(BF16)
        normed_grad = mixed_grad * gate
        out_grad_ref[:, lanes] = (scale * (normed_grad - normed * head_mean(normed_grad * normed, ones))).astype(BF16)


def open_back(half, out_grad, w_out):
    gate, attended = half[5:7]
    rows, columns = gate.shape
    width = out_grad.shape[1]
    return call(
        open_back_kernel,
        (rows // TILE,),
        (gate, attended, out_grad, w_out),
        [row_tile(columns), row_tile(columns), row_tile(width), whole(w_out)],
        [shaped(rows, columns)] * 2,
        [row_tile(columns)] * 2,
        2 * rows * columns * width,
    )


def attend_back_kernel(
    rate_ref, q_ref, sq_ref, k_ref, sk_ref, v_ref, grad_ref, dq_ref, dk_ref, dv_ref, states
):
    rates, query_decay, key_decay, chunk_decay = decays(rate_ref)
    first = head_lanes()
    same = same_head()
    tables = [within_table(rate) for rate in rates]
    flipped = [within_table(rate, True) for rate in rates]
    masks = [jnp.where(first, 1.0, 0.0).astype(BF16), jnp.where(first, 0.0, 1.0).astype(BF16)]
    chunks = q_ref.shape[0] // CHUNK
    state = jnp.zeros((PAIR, PAIR), F32)
    for index in range(chunks):
        rows = pl.ds(index * CHUNK, CHUNK)
        states[index] = state.astype(BF16)
        if index < chunks - 1:
            keys = (k_ref[rows, :].astype(F32) * key_decay).T.astype(BF16)
            state = chunk_decay * state + jnp.where(same, matmul(keys, v_ref[rows, :]), 0.0)
    carry = jnp.zeros((PAIR, PAIR), F32)
    for index in reversed(range(chunks)):
        rows = pl.ds(index * CHUNK, CHUNK)
        q, k, v, grad = q_ref[rows, :], k_ref[rows, :], v_ref[rows, :], grad_ref[rows, :]
        narrow = carry.astype(BF16)
        dq = times_transpose(grad, states[index]) * query_decay
        dk = times_transpose(v, narrow) * key_decay
        dv = matmul(k, narrow) * key_decay
        for mask, table, turned in zip(masks, tables, flipped):
            q_one, grad_one = q * mask, grad * mask
            weights = (times_transpose(k, q_one) * turned).astype(BF16)
            dv = dv + matmul(weights, grad_one)
            dq = dq + matmul((times_transpose(grad_one, v) * table).astype(BF16), k * mask)
            dk = dk + matmul((times_transpose(v, grad_one) * turned).astype(BF16), q_one)
        dq_ref[rows, :] = (dq * sq_ref[rows, :].astype(F32)).astype(BF16)
        dk_ref[rows, :] = (dk * sk_ref[rows, :].astype(F32)).astype(BF16)
        dv_ref[rows, :] = dv.astype(BF16)
        if index > 0:
            turned_q = q.astype(F32).T.astype(BF16)
            decayed = (grad.astype(F32) * query_decay).astype(BF16)
            carry = chunk_decay * carry + jnp.where(same, matmul(turned_q, decayed), 0.0)


def attend_back(half, attended_grad):
    q, sq, k, sk, v, _, _, rates = half
    rows, columns = q.shape
    return call(
        attend_back_kernel,
        (columns // PAIR,),
        (rates, q, sq, k, sk, v, attended_grad),
        [pl.BlockSpec(memory_space=pltpu.SMEM)] + [pair_spec(rows)] * 6,
        [shaped(rows, columns)] * 3,
        [pair_spec(rows)] * 3,
        30 * rows * columns * CHUNK,
        scratch=[pltpu.VMEM((rows // CHUNK, PAIR, PAIR), BF16)],
    )


def glu_parts(hidden, out_grad, wg_ref, wu_ref, wd_ref, columns, turned=False):
    gate_pre = matmul(hidden, wg_ref[:, columns])
    up_pre = matmul(hidden, wu_ref[:, columns])
    if turned:
        glu_grad = matmul(out_grad, wd_ref[:, columns])
    else:
        glu_grad = times_transpose(out_grad, wd_ref[columns, :])
    logistic = jax.nn.sigmoid(gate_pre)
    act = gate_pre * logistic
    glu = (act * up_pre).astype(BF16)
    up_grad = (glu_grad * act).astype(BF16)
    gate_grad = (glu_grad * up_pre * (logistic * (1.0 + gate_pre * (1.0 - logistic)))).astype(BF16)
    return glu, gate_grad, up_grad


def unit_slices(units):
    step = 512
    return [slice(low, min(low + step, units)) for low in range(0, units, step)]


def middle_kernel(
    inputs_ref, live_ref, dy_ref, mixed_a_ref, mixed_b_ref, wo_a_ref, wo_b_ref, gain_ref, wg_ref, wu_ref, wd_ref,
    residual_ref, hidden_ref, glu_ref, gate_grad_ref, up_grad_ref, branch_ref, back_ref,
):
    live = live_ref[...]
    branch = matmul(mixed_a_ref[...], wo_a_ref[...]) + matmul(mixed_b_ref[...], wo_b_ref[...])
    residual = inputs_ref[...].astype(F32) + live * branch
    residual_ref[...] = residual
    scale = lax.rsqrt(row_mean(residual * residual) + EPS)
    hidden = (residual * scale * gain_ref[...].astype(F32)).astype(BF16)
    hidden_ref[...] = hidden
    out_grad = (live * dy_ref[...].astype(F32)).astype(BF16)
    units = wg_ref.shape[1]
    for columns in unit_slices(units):
        glu, gate_grad, up_grad = glu_parts(hidden, out_grad, wg_ref, wu_ref, wd_ref, columns)
        glu_ref[:, columns] = glu
        gate_grad_ref[:, columns] = gate_grad
        up_grad_ref[:, columns] = up_grad
    branch_ref[...] = matmul(glu_ref[...], wd_ref[...])
    back_ref[...] = times_transpose(gate_grad_ref[...], wg_ref[...]) + times_transpose(up_grad_ref[...], wu_ref[...])


def middle(inputs, live, dy, mixed, outs, gain, glus):
    rows, width = inputs.shape
    heads = mixed[0].shape[1]
    units = glus[0].shape[1]
    return call(
        middle_kernel,
        (rows // TILE,),
        (inputs, live, dy, *mixed, *outs, gain, *glus),
        [row_tile(width), row_tile(1), row_tile(width), row_tile(heads), row_tile(heads)]
        + [whole(w) for w in (*outs, gain, *glus)],
        [shaped(rows, width, F32), shaped(rows, width)]
        + [shaped(rows, units)] * 3
        + [shaped(rows, width, F32)] * 2,
        [row_tile(width)] * 2 + [row_tile(units)] * 3 + [row_tile(width)] * 2,
        2 * rows * width * (2 * heads + 6 * units),
    )


def norm_back(grad, normed, scale):
    return scale * (grad - normed * row_mean(grad * normed))


def middle_back_kernel(
    residual_ref, hidden_ref, live_ref, dy_ref, branch_ref, back_ref, gain_ref, wg_ref, wu_ref, wd_ref,
    result_ref, mid_ref, grad_ref, gain_grad_ref, glu_buf, gate_buf, up_buf,
):
    live = live_ref[...]
    dy = dy_ref[...].astype(F32)
    hidden = hidden_ref[...]
    out_grad = (live * dy).astype(BF16)
    for columns in unit_slices(wg_ref.shape[1]):
        glu_buf[:, columns], gate_buf[:, columns], up_buf[:, columns] = glu_parts(
            hidden, out_grad, wg_ref, wu_ref, wd_ref, columns, True
        )
    residual = residual_ref[...]
    branch = branch_ref[...] + times_transpose(glu_buf[...], wd_ref[...])
    result_ref[...] = (residual + live * branch).astype(BF16)
    back = back_ref[...] + times_transpose(gate_buf[...], wg_ref[...]) + times_transpose(up_buf[...], wu_ref[...])
    scale = lax.rsqrt(row_mean(residual * residual) + EPS)
    normed = residual * scale

    @pl.when(pl.program_id(0) == 0)
    def _():
        gain_grad_ref[...] = jnp.zeros_like(gain_grad_ref)

    gain_grad_ref[...] += jnp.sum(back * normed, axis=0, keepdims=True)
    mid = dy + norm_back(back * gain_ref[...].astype(F32), normed, scale)
    mid_ref[...] = mid
    grad_ref[...] = (live * mid).astype(BF16)


def middle_back(residual, hidden, live, dy, branch, back, gain, glus):
    rows, width = hidden.shape
    units = glus[0].shape[1]
    return call(
        middle_back_kernel,
        (rows // TILE,),
        (residual, hidden, live, dy, branch, back, gain, *glus),
        [row_tile(width), row_tile(width), row_tile(1)]
        + [row_tile(width)] * 3
        + [whole(w) for w in (gain, *glus)],
        [shaped(rows, width), shaped(rows, width, F32), shaped(rows, width), shaped(1, width, F32)],
        [row_tile(width)] * 3 + [pl.BlockSpec((1, width), lambda step: (0, 0))],
        2 * rows * width * 6 * units,
        scratch=[pltpu.VMEM((TILE, units), BF16)] * 3,
    )


def first_back_kernel(inputs_ref, mid_ref, gain_ref, *refs):
    grads, weights, (result_ref, gain_grad_ref) = refs[:8], refs[8:16], refs[16:]
    back = times_transpose(grads[0][...], weights[0][...])
    for grad, weight in zip(grads[1:], weights[1:]):
        back = back + times_transpose(grad[...], weight[...])
    wide = inputs_ref[...].astype(F32)
    scale = lax.rsqrt(row_mean(wide * wide) + EPS)
    normed = wide * scale

    @pl.when(pl.program_id(0) == 0)
    def _():
        gain_grad_ref[...] = jnp.zeros_like(gain_grad_ref)

    gain_grad_ref[...] += jnp.sum(back * normed, axis=0, keepdims=True)
    result_ref[...] = (mid_ref[...] + norm_back(back * gain_ref[...].astype(F32), normed, scale)).astype(BF16)


def first_back(inputs, mid, gain, grads, weights):
    rows, width = inputs.shape
    columns = weights[0].shape[1]
    return call(
        first_back_kernel,
        (rows // TILE,),
        (inputs, mid, gain, *grads, *weights),
        [row_tile(width), row_tile(width), whole(gain)]
        + [row_tile(columns)] * 8
        + [whole(w) for w in weights],
        [shaped(rows, width), shaped(1, width, F32)],
        [row_tile(width), pl.BlockSpec((1, width), lambda step: (0, 0))],
        2 * rows * width * columns * 8,
    )


def product_kernel(count, first, came_first, column, plan, left_refs, right_refs, came_ref, out_ref):
    tile = min(TILE, count)
    for low in range(0, count, tile):
        for left, right, start in plan:
            stop = start + right_refs[right].shape[1]
            total = matmul(left_refs[left][first + low : first + low + tile, :], right_refs[right][...])
            if came_ref is not None:
                total = total + came_ref[came_first + low : came_first + low + tile, column + start : column + stop]
            out_ref[low : low + tile, start:stop] = total


def product(lefts, rights, first, count, came=None, came_first=0, column=0):
    distinct = []
    plan = []
    start = 0
    for which, (left, right) in enumerate(zip(lefts, rights)):
        if not any(left is seen for seen in distinct):
            distinct.append(left)
        plan.append(([left is seen for seen in distinct].index(True), which, start))
        start += right.shape[1]
    n_left, n_right = len(distinct), len(rights)

    def body(*refs):
        came_ref = None if came is None else refs[n_left + n_right]
        product_kernel(
            count, first, came_first, column, plan, refs[:n_left], refs[n_left : n_left + n_right], came_ref, refs[-1]
        )

    ins = [*distinct, *rights] + ([] if came is None else [came])
    vmem = pl.BlockSpec(memory_space=pltpu.VMEM)
    return pl.pallas_call(
        body,
        in_specs=[vmem] * len(ins),
        out_specs=vmem,
        out_shape=shaped(count, start, F32),
        cost_estimate=pl.CostEstimate(
            flops=2 * count * lefts[0].shape[1] * start // COST, bytes_accessed=1024, transcendentals=0
        ),
        compiler_params=pltpu.CompilerParams(vmem_limit_bytes=10 * MIB),
    )(*ins)


def products_kernel(left_of, n_left, *refs):
    lefts, rights, out_ref = refs[:n_left], refs[n_left:-1], refs[-1]
    start = 0
    for left, right in zip(left_of, rights):
        stop = start + right.shape[1]
        out_ref[:, start:stop] = matmul(lefts[left][...], right[...])
        start = stop


def products(lefts, left_of, rights):
    rows, depth = lefts[0].shape
    columns = sum(right.shape[1] for right in rights)
    return call(
        functools.partial(products_kernel, left_of, len(lefts)),
        (rows // TILE,),
        (*lefts, *rights),
        [row_tile(depth)] * len(lefts) + [whole(right) for right in rights],
        shaped(rows, columns, F32),
        row_tile(columns),
        2 * rows * depth * columns,
    )


def flip_kernel(array_ref, *refs):
    out_ref = refs[-1]
    for low in range(0, array_ref.shape[1], PAIR):
        values = array_ref[:, low : low + PAIR].astype(F32)
        if len(refs) == 2:
            values = values * refs[0][...]
        out_ref[low : low + PAIR, :] = values.T.astype(BF16)


def flip(array, live=None):
    rows, width = array.shape
    lives = () if live is None else (live,)
    vmem = pl.BlockSpec(memory_space=pltpu.VMEM)
    return pl.pallas_call(
        flip_kernel,
        out_shape=shaped(width, rows),
        in_specs=[vmem] * (1 + len(lives)),
        out_specs=vmem,
        cost_estimate=pl.CostEstimate(flops=1024, bytes_accessed=1024, transcendentals=0),
        compiler_params=pltpu.CompilerParams(vmem_limit_bytes=10 * MIB),
    )(array, *lives)


def turn_kernel(near_first, place_ref, array_ref, *refs):
    out_ref, turned = refs[-2:]
    core, chip = place_ref[0] % 2, place_ref[0] // 2
    part = out_ref.shape[1] // 8
    for step in range(8):
        high, middle_bit, low = step // 4, (step // 2) % 2, step % 2
        across, near, far = (low, high, middle_bit) if near_first else (high, middle_bit, low)
        block = chip ^ (far * 4 + near * 2 + across)
        values = array_ref[:, pl.ds(pl.multiple_of(block * 2 * part, 2 * part), 2 * part)].astype(F32)
        if len(refs) == 3:
            values = values * refs[0][...]
        turned[...] = values.T
        rows = slice(step * part, (step + 1) * part)
        out_ref[0, rows, :] = turned[pl.ds(pl.multiple_of(core * part, part), part), :].astype(BF16)
        out_ref[1, rows, :] = turned[pl.ds(pl.multiple_of((1 - core) * part, part), part), :].astype(BF16)


def turn(array, place, near_first=False, live=None):
    rows, width = array.shape
    lives = () if live is None else (live,)
    vmem = pl.BlockSpec(memory_space=pltpu.VMEM)
    out = pl.pallas_call(
        functools.partial(turn_kernel, near_first),
        out_shape=jax.ShapeDtypeStruct((2, width // 2, rows), BF16),
        in_specs=[pl.BlockSpec(memory_space=pltpu.SMEM)] + [vmem] * (1 + len(lives)),
        out_specs=vmem,
        scratch_shapes=[pltpu.VMEM((width // 8, rows), F32)],
        cost_estimate=pl.CostEstimate(flops=1024, bytes_accessed=1024, transcendentals=0),
        compiler_params=pltpu.CompilerParams(vmem_limit_bytes=10 * MIB),
    )(place, array, *lives)
    return out.reshape(width, rows)


CORE, ACROSS_X, NEAR_Z, FAR_Z = 1, 2, 4, 8


def hold(*trees):
    return lax.optimization_barrier(trees)


def swap_dp(array, bit, size=16):
    return lax.ppermute(array, "dp", [(place, place ^ bit) for place in range(size)])


def swap_tensor(array):
    return lax.ppermute(array, "tensor", [(0, 1), (1, 0)])


def cut_kernel(count, place_ref, *refs):
    out_ref = refs[-1]
    part = refs[0].shape[0]
    for which in range(count):
        out_ref[which * part : (which + 1) * part, :] = refs[which][...].astype(F32)


def cut(weights, place, parts, flips=(0,)):
    rows, columns = weights[0].shape
    part = rows // parts
    count = len(weights) * len(flips)
    specs = [
        pl.BlockSpec((part, columns), lambda step, ref, bits=bits: (ref[0] ^ bits, 0))
        for bits in flips
        for _ in weights
    ]
    return pl.pallas_call(
        functools.partial(cut_kernel, count),
        out_shape=shaped(count * part, columns, F32),
        grid_spec=pltpu.PrefetchScalarGridSpec(
            num_scalar_prefetch=1,
            grid=(1,),
            in_specs=specs,
            out_specs=pl.BlockSpec((count * part, columns), lambda step, ref: (0, 0)),
        ),
        cost_estimate=pl.CostEstimate(flops=1024, bytes_accessed=1024, transcendentals=0),
        compiler_params=pltpu.CompilerParams(vmem_limit_bytes=20 * MIB),
    )(place, *(list(weights) * len(flips)))


def spread_kernel(wide_ref, *outs):
    part = outs[0].shape[0]
    for which, out in enumerate(outs):
        out[...] = wide_ref[which * part : (which + 1) * part, :].astype(BF16)


def spread(wide, count):
    rows, columns = wide.shape
    return call(
        spread_kernel,
        (16,),
        (wide,),
        [row_tile(columns, rows // 16)],
        [shaped(rows // count, columns)] * count,
        [row_tile(columns, rows // 16 // count)] * count,
        1024,
    )


def place_kernel(count, place_ref, *refs):
    pieces, outs = refs[:8], refs[8:]
    place = place_ref[0]
    part = outs[0].shape[0] // 8
    for index in range(8):
        target = place ^ index
        for which in range(count):
            outs[which][pl.ds(pl.multiple_of(target * part, part), part), :] = pieces[index][
                which * part : (which + 1) * part, :
            ].astype(BF16)


def put(pieces, count, place):
    height, columns = pieces[0].shape
    rows = 8 * height // count
    once = dict(pipeline_mode=pl.Buffered(1))
    return pl.pallas_call(
        functools.partial(place_kernel, count),
        out_shape=[shaped(rows, columns)] * count,
        grid_spec=pltpu.PrefetchScalarGridSpec(
            num_scalar_prefetch=1,
            grid=(1,),
            in_specs=[pl.BlockSpec((height, columns), lambda step, ref: (0, 0), **once)] * 8,
            out_specs=[pl.BlockSpec((rows, columns), lambda step, ref: (0, 0), **once)] * count,
        ),
        cost_estimate=pl.CostEstimate(flops=1024, bytes_accessed=1024, transcendentals=0),
        compiler_params=pltpu.CompilerParams(vmem_limit_bytes=20 * MIB),
    )(place, *pieces)


def cast_kernel(wide_ref, out_ref):
    out_ref[...] = wide_ref[...].astype(BF16)


def cast_weight(wide):
    rows, columns = wide.shape
    spec = pl.BlockSpec((rows // 8, columns), lambda row: (row, 0))
    return pl.pallas_call(
        cast_kernel, grid=(8,), out_shape=jax.ShapeDtypeStruct(wide.shape, BF16), in_specs=[spec], out_specs=spec
    )(wide)


def relative_rows(array, dp_place, order):
    blocks = array.reshape(2, 2, 2, 2, array.shape[0] // 16, array.shape[1])
    for axis, bit in enumerate((FAR_Z, NEAR_Z, ACROSS_X, CORE)):
        blocks = jnp.where((dp_place & bit) > 0, jnp.flip(blocks, axis), blocks)
    axes = {FAR_Z: 0, NEAR_Z: 1, ACROSS_X: 2, CORE: 3}
    return blocks.transpose([axes[bit] for bit in order] + [4, 5]).reshape(array.shape)


ORDER_X = (CORE, ACROSS_X, NEAR_Z, FAR_Z)
ORDER_Z = (CORE, NEAR_Z, FAR_Z, ACROSS_X)


class Scatter:
    def __init__(self, lefts, rights, order, came, column):
        self.order, self.stage = order, 1
        part = lefts[0].shape[0] // 4
        self.send = product(lefts, rights, part, part, came, part, column)
        self.kept = product(lefts, rights, 0, part, came, 0, column)

    def go(self):
        self.came = swap_dp(self.send, self.order[self.stage])
        self.stage += 1

    def step(self):
        half = self.kept.shape[0] // 2
        self.send = self.kept[half:] + self.came[half:]
        self.kept = self.kept[:half] + self.came[:half]
        self.go()

    def total(self):
        return self.kept + self.came


def scatter_vector(vector, dp_place):
    kept = relative_rows(vector, dp_place, ORDER_X)
    for bit in ORDER_X:
        half = kept.shape[0] // 2
        kept = kept[:half] + swap_dp(kept[half:], bit)
    return kept


def rates_of(side, local_heads):
    head_ids = jnp.arange(local_heads)
    return tuple(
        jnp.exp2(-8.0 * ((which * local_heads + head_ids).astype(F32) + 1.0) / HEADS)
        for which in (side, 1 - side)
    )


def forward_half(hidden, live, weights, rates):
    parts = project(hidden, live, weights)
    q, sq, k, sk, v, gate = parts
    attended, mixed = attend(q, k, v, gate, rates)
    return (*parts, attended, rates), mixed


def shards_plain(
    inputs, lengths, gain_attn, w_query, w_key, w_value, w_gate_attn, w_out, gain_ffn, w_gate, w_up, w_down, cotangent
):
    own = (w_query, w_key, w_value, w_gate_attn, w_out, w_gate, w_up, w_down)
    others = [cast_weight(swap_tensor(weight.astype(F32))) for weight in own]
    rates = rates_of(lax.axis_index("tensor"), w_query.shape[1] // HEAD_DIM)
    positions = jnp.arange(inputs.shape[0], dtype=jnp.int32)
    live = (positions < lengths[0]).astype(F32)[:, None]
    gain_one, gain_two = gain_attn.reshape(1, -1), gain_ffn.reshape(1, -1)
    out_grad = (live * cotangent.astype(F32)).astype(BF16)
    hidden_one = first_norm(inputs, gain_one)
    half_a, mixed_a = forward_half(hidden_one, live, own[:4], rates[0])
    half_b, mixed_b = forward_half(hidden_one, live, others[:4], rates[1])
    residual, hidden_two, glu, gate_grad, up_grad, branch, back = middle(
        inputs, live, cotangent, (mixed_a, mixed_b), (w_out, others[4]), gain_two, own[5:]
    )
    result, mid_grad, attn_out_grad, gain_two_grad = middle_back(
        residual, hidden_two, live, cotangent, branch, back, gain_two, (others[5], others[6], others[7].T)
    )
    open_a, gate_a = open_back(half_a, attn_out_grad, w_out)
    open_b, gate_b = open_back(half_b, attn_out_grad, others[4])
    back_a = (*attend_back(half_a, open_a), gate_a)
    back_b = (*attend_back(half_b, open_b), gate_b)
    input_grad, gain_one_grad = first_back(
        inputs, mid_grad, gain_one, (*back_a, *back_b), (*own[:4], *others[:4])
    )
    pairs = [(hidden_one, grad) for grad in back_a]
    pairs += [(attn_out_grad, mixed_a), (hidden_two, gate_grad), (hidden_two, up_grad), (out_grad, glu)]
    sums = [
        lax.psum_scatter(matmul(left.T, right), "dp", scatter_dimension=0, tiled=True) for left, right in pairs
    ]
    gains = [lax.psum_scatter(grad[0], "dp", scatter_dimension=0, tiled=True) for grad in (gain_one_grad, gain_two_grad)]
    return (result, input_grad, gains[0], *sums[:4], sums[4].T, gains[1], sums[5], sums[6], sums[7].T)


def shards_here(
    inputs, lengths, gain_attn, w_query, w_key, w_value, w_gate_attn, w_out, gain_ffn, w_gate, w_up, w_down, cotangent
):
    seq_rows = inputs.shape[0]
    side = lax.axis_index("tensor")
    dp_place = lax.axis_index("dp")
    place = (dp_place % 8).reshape(1)
    rates = rates_of(side, w_query.shape[1] // HEAD_DIM)
    positions = jnp.arange(seq_rows, dtype=jnp.int32)
    live = (positions < lengths[0]).astype(F32)[:, None]
    gain_one = gain_attn.reshape(1, -1)
    gain_two = gain_ffn.reshape(1, -1)

    proj = (w_query, w_key, w_value, w_gate_attn)
    whole_place = dp_place.reshape(1)
    y1 = swap_tensor(cut(proj, place, 8))
    features = w_down.shape[1] // 16
    down_piece = lax.dynamic_slice_in_dim(w_down, dp_place * features, features, 1).T
    glu_cut = jnp.concatenate([cut((w_gate, w_up), whole_place, 16), down_piece.astype(F32)], axis=0)
    out_cut = cut((w_out,), place, 8, (0, 6))
    hidden_one = first_norm(inputs, gain_one)
    parts = project(hidden_one, live, proj)

    y1, parts, glu_cut, out_cut = hold(y1, parts, glu_cut, out_cut)
    x1, z1, y1c = swap_dp(y1, ACROSS_X), swap_dp(y1, NEAR_Z), swap_dp(y1, CORE)
    glu_cut = swap_tensor(glu_cut)
    q, sq, k, sk, v, gate = parts
    attended, mixed_a = attend(q, k, v, gate, rates[0])
    half_a = (*parts, attended, rates[0])
    dy_t = flip(cotangent, live)

    x1, z1, y1c, glu_cut, mixed_a, dy_t, hidden_one, out = hold(x1, z1, y1c, glu_cut, mixed_a, dy_t, hidden_one, out_cut)
    glu_wide = lax.all_gather(glu_cut, "dp", axis=0, tiled=True)
    part = y1.shape[0] // 2
    from_x, from_z = swap_dp(z1[:part], ACROSS_X), swap_dp(x1[part:], NEAR_Z)
    x1c, z1c = swap_dp(x1, CORE), swap_dp(z1, CORE)
    out = swap_tensor(out)
    hidden_one_t = turn(hidden_one, whole_place)
    hidden_one_tz = turn(hidden_one, whole_place, near_first=True)

    from_x, from_z, x1c, z1c, out, hidden_one_t, hidden_one_tz = hold(
        from_x, from_z, x1c, z1c, out, hidden_one_t, hidden_one_tz
    )
    y2 = jnp.concatenate([from_x, from_z], axis=0)
    y2c = swap_dp(y2, CORE)
    part = out.shape[0] // 2
    ox, oz, out_c = swap_dp(out[:part], ACROSS_X), swap_dp(out[:part], NEAR_Z), swap_dp(out, CORE)
    proj_b = put((y1, y1c, x1, x1c, z1, z1c, y2, y2c), 4, place)
    parts = project(hidden_one, live, proj_b)

    parts, ox, oz, out_c = hold(parts, ox, oz, out_c)
    out_xz = swap_dp(jnp.concatenate([ox, oz], axis=0), CORE)
    q, sq, k, sk, v, gate = parts
    attended, mixed_b = attend(q, k, v, gate, rates[1])
    half_b = (*parts, attended, rates[1])

    mixed_b, out_xz = hold(mixed_b, out_xz)
    (w_out_b,) = put(
        (out[:part], out_c[:part], ox, out_xz[:part], oz, out_xz[part:], out[part:], out_c[part:]), 1, place
    )
    residual, hidden_two, glu, gate_grad, up_grad, branch, back = middle(
        inputs, live, cotangent, (mixed_a, mixed_b), (w_out, w_out_b), gain_two, (w_gate, w_up, w_down)
    )
    wide = products((dy_t, flip(hidden_two)), (0, 1, 1), (glu, gate_grad, up_grad))

    residual, wide = hold(residual, wide)
    units = glu.shape[1]
    ffn_sums = lax.psum_scatter(wide, "dp", scatter_dimension=0, tiled=True)
    result, mid_grad, attn_out_grad, gain_two_grad = middle_back(
        residual, hidden_two, live, cotangent, branch, back, gain_two, spread(glu_wide, 3)
    )

    half = dy_t.shape[0] // 2
    open_a, gate_a = open_back(half_a, attn_out_grad, w_out)
    attn_out_grad_t = turn(attn_out_grad, whole_place, near_first=True)
    lefts, rights = (attn_out_grad_t, hidden_one_tz), (mixed_a, gate_a)
    came = swap_dp(product(lefts, rights, half, half), CORE)

    open_a, came, attn_out_grad = hold(open_a, came, attn_out_grad)
    second = Scatter(lefts, rights, ORDER_Z, came, 0)
    second.go()
    own = attend_back(half_a, open_a)

    own, attn_out_grad = hold(own, attn_out_grad)
    lefts = (hidden_one_t,) * 3
    came = swap_dp(product(lefts, own, half, half), CORE)
    open_b, gate_b = open_back(half_b, attn_out_grad, w_out_b)

    open_b, came = hold(open_b, came)
    first = Scatter(lefts, own, ORDER_X, came, 0)
    first.go()
    other = attend_back(half_b, open_b)

    own, other = (*own, gate_a), (*other, gate_b)
    input_grad, gain_one_grad = first_back(inputs, mid_grad, gain_one, (*own, *other), (*proj, *proj_b))

    input_grad, first.came, second.came, gain_one_grad = hold(input_grad, first.came, second.came, gain_one_grad)
    first.step()
    second.step()
    gains = scatter_vector(jnp.concatenate([gain_one_grad, gain_two_grad], axis=0).T, dp_place)
    first.came, second.came, gains = hold(first.came, second.came, gains)
    first.step()
    second.step()
    first_sum, second_sum = first.total(), second.total()
    first_sum, second_sum, ffn_sums = hold(first_sum, second_sum, ffn_sums)
    width = w_query.shape[1]
    return (
        result,
        input_grad,
        gains[:, 0],
        first_sum[:, :width],
        first_sum[:, width : 2 * width],
        first_sum[:, 2 * width :],
        second_sum[:, width:],
        second_sum[:, :width].T,
        gains[:, 1],
        ffn_sums[:, units : 2 * units],
        ffn_sums[:, 2 * units :],
        ffn_sums[:, :units].T,
    )


def solution(mesh):
    placed = (
        P("dp", None),
        P("dp"),
        P(),
        P(None, "tensor"),
        P(None, "tensor"),
        P(None, "tensor"),
        P(None, "tensor"),
        P("tensor", None),
        P(),
        P(None, "tensor"),
        P(None, "tensor"),
        P("tensor", None),
        P("dp", None),
    )
    return jax.shard_map(
        shards_here if mesh.shape["dp"] == 16 else shards_plain,
        mesh=mesh,
        in_specs=placed,
        out_specs=(
            P("dp", None),
            P("dp", None),
            P("dp"),
            P("dp", "tensor"),
            P("dp", "tensor"),
            P("dp", "tensor"),
            P("dp", "tensor"),
            P("tensor", "dp"),
            P("dp"),
            P("dp", "tensor"),
            P("dp", "tensor"),
            P("tensor", "dp"),
        ),
        check_vma=False,
    )
```

```python
import functools

import jax
import jax.numpy as jnp
from jax import lax
from jax.experimental import pallas as pl
from jax.experimental.pallas import tpu as pltpu
from jax.sharding import PartitionSpec as P

HEADS = 16
HEAD_DIM = 64
BLOCK = 512
EPS = 1e-06
HIGHEST = lax.Precision.HIGHEST
F32 = jnp.float32
BF16 = jnp.bfloat16


def matmul(left, right):
    return jnp.dot(left, right, preferred_element_type=F32)


def times_transpose(left, right):
    return lax.dot_general(left, right, (((1,), (1,)), ((), ())), preferred_element_type=F32)


def row_mean(array):
    return jnp.mean(array, axis=1, keepdims=True)


MIB = 2**20
COST = 1000
TILE = 256
CHUNK = 256
PAIR = 2 * HEAD_DIM


def whole(array):
    return pl.BlockSpec(array.shape, lambda *_: (0,) * array.ndim, pipeline_mode=pl.Buffered(1))


def row_tile(columns, rows=TILE):
    return pl.BlockSpec((rows, columns), lambda step: (step, 0))


def call(body, grid, ins, in_specs, outs, out_specs, flops, scratch=(), limit=34):
    return pl.pallas_call(
        body,
        grid=grid,
        in_specs=in_specs,
        out_specs=out_specs,
        out_shape=outs,
        scratch_shapes=scratch,
        cost_estimate=pl.CostEstimate(flops=int(flops) // COST, bytes_accessed=1024, transcendentals=0),
        compiler_params=pltpu.CompilerParams(vmem_limit_bytes=limit * MIB),
    )(*ins)


def shaped(rows, columns, kind=BF16):
    return jax.ShapeDtypeStruct((rows, columns), kind)


def norm_kernel(inputs_ref, gain_ref, hidden_ref):
    wide = inputs_ref[...].astype(F32)
    scale = lax.rsqrt(row_mean(wide * wide) + EPS)
    hidden_ref[...] = (wide * scale * gain_ref[...].astype(F32)).astype(BF16)


def first_norm(inputs, gain):
    rows, width = inputs.shape
    return call(
        norm_kernel,
        (rows // TILE,),
        (inputs, gain),
        [row_tile(width), whole(gain)],
        shaped(rows, width),
        row_tile(width),
        rows * width * 8,
    )


def project_kernel(hidden_ref, live_ref, wq_ref, wk_ref, wv_ref, wg_ref, q_ref, sq_ref, k_ref, sk_ref, v_ref, gate_ref):
    hidden = hidden_ref[...]
    live = live_ref[...]

    def activate(value):
        small = jnp.exp(-jnp.abs(value))
        share = 1.0 / (1.0 + small)
        return jnp.maximum(value, 0.0) + jnp.log1p(small), jnp.where(value >= 0.0, share, small * share)

    positive, slope = activate(matmul(hidden, wq_ref[...]))
    q_ref[...] = positive.astype(BF16)
    sq_ref[...] = slope.astype(BF16)
    positive, slope = activate(matmul(hidden, wk_ref[...]))
    k_ref[...] = (positive * live).astype(BF16)
    sk_ref[...] = (slope * live).astype(BF16)
    v_ref[...] = matmul(hidden, wv_ref[...]).astype(BF16)
    gate_ref[...] = jax.nn.sigmoid(matmul(hidden, wg_ref[...]))


def project(hidden, live, weights):
    rows, width = hidden.shape
    columns = weights[0].shape[1]
    narrow = shaped(rows, columns)
    return call(
        project_kernel,
        (rows // TILE,),
        (hidden, live, *weights),
        [row_tile(width), row_tile(1)] + [whole(w) for w in weights],
        [narrow] * 5 + [shaped(rows, columns, F32)],
        [row_tile(columns)] * 6,
        8 * rows * width * columns,
    )


def head_lanes():
    return lax.broadcasted_iota(jnp.int32, (1, PAIR), 1) < HEAD_DIM


def same_head():
    rows = lax.broadcasted_iota(jnp.int32, (PAIR, PAIR), 0) < HEAD_DIM
    columns = lax.broadcasted_iota(jnp.int32, (PAIR, PAIR), 1) < HEAD_DIM
    return rows == columns


def head_mean(array, ones):
    high = array.astype(BF16)
    low = (array - high.astype(F32)).astype(BF16)
    return (matmul(high, ones) + matmul(low, ones)) * (1.0 / HEAD_DIM)


def decays(rate_ref):
    pair = pl.program_id(0)
    rates = (rate_ref[2 * pair], rate_ref[2 * pair + 1])
    lane_rate = jnp.where(head_lanes(), rates[0], rates[1])
    place = lax.broadcasted_iota(jnp.int32, (CHUNK, 1), 0).astype(F32)
    query_decay = jnp.exp(-lane_rate * (place + 1.0))
    key_decay = jnp.exp(-lane_rate * (CHUNK - 1.0 - place))
    chunk_decay = jnp.exp(-lane_rate * CHUNK)
    return rates, query_decay, key_decay, chunk_decay


def within_table(rate, flipped=False):
    rows = lax.broadcasted_iota(jnp.int32, (CHUNK, CHUNK), 0)
    columns = lax.broadcasted_iota(jnp.int32, (CHUNK, CHUNK), 1)
    spread = columns - rows if flipped else rows - columns
    kept = spread >= 0
    return jnp.where(kept, jnp.exp(-rate * jnp.where(kept, spread, 0).astype(F32)), 0.0)


def attend_kernel(rate_ref, q_ref, k_ref, v_ref, gate_ref, attended_ref, mixed_ref):
    rates, query_decay, key_decay, chunk_decay = decays(rate_ref)
    first = head_lanes()
    same = same_head()
    ones = jnp.where(same, 1.0, 0.0).astype(BF16)
    tables = [within_table(rate) for rate in rates]
    masks = [jnp.where(first, 1.0, 0.0).astype(BF16), jnp.where(first, 0.0, 1.0).astype(BF16)]
    state = jnp.zeros((PAIR, PAIR), F32)
    for index in range(q_ref.shape[0] // CHUNK):
        rows = pl.ds(index * CHUNK, CHUNK)
        q, k, v = q_ref[rows, :], k_ref[rows, :], v_ref[rows, :]
        attended = matmul(q, state.astype(BF16)) * query_decay
        for mask, table in zip(masks, tables):
            weights = (times_transpose(q * mask, k) * table).astype(BF16)
            attended = attended + matmul(weights, v * mask)
        keys = (k.astype(F32) * key_decay).T.astype(BF16)
        state = chunk_decay * state + jnp.where(same, matmul(keys, v), 0.0)
        scale = lax.rsqrt(head_mean(attended * attended, ones) + EPS)
        attended_ref[rows, :] = attended
        mixed_ref[rows, :] = (attended * scale * gate_ref[rows, :]).astype(BF16)


def pair_spec(rows):
    return pl.BlockSpec((rows, PAIR), lambda pair: (0, pair))


def attend(q, k, v, gate, rates):
    rows, columns = q.shape
    return call(
        attend_kernel,
        (columns // PAIR,),
        (rates, q, k, v, gate),
        [pl.BlockSpec(memory_space=pltpu.SMEM)] + [pair_spec(rows)] * 4,
        [shaped(rows, columns, F32), shaped(rows, columns)],
        [pair_spec(rows)] * 2,
        12 * rows * columns * CHUNK,
    )


def open_back_kernel(gate_ref, attended_ref, grad_ref, wo_ref, out_grad_ref, dg_ref):
    ones = jnp.where(same_head(), 1.0, 0.0).astype(BF16)
    wide = times_transpose(grad_ref[...], wo_ref[...])
    for low in range(0, wide.shape[1], PAIR):
        lanes = slice(low, low + PAIR)
        mixed_grad, attended, gate = wide[:, lanes], attended_ref[:, lanes], gate_ref[:, lanes]
        scale = lax.rsqrt(head_mean(attended * attended, ones) + EPS)
        normed = attended * scale
        dg_ref[:, lanes] = (mixed_grad * normed * gate * (1.0 - gate)).astype(BF16)
        normed_grad = mixed_grad * gate
        out_grad_ref[:, lanes] = (scale * (normed_grad - normed * head_mean(normed_grad * normed, ones))).astype(BF16)


def open_back(half, out_grad, w_out):
    gate, attended = half[5:7]
    rows, columns = gate.shape
    width = out_grad.shape[1]
    return call(
        open_back_kernel,
        (rows // TILE,),
        (gate, attended, out_grad, w_out),
        [row_tile(columns), row_tile(columns), row_tile(width), whole(w_out)],
        [shaped(rows, columns)] * 2,
        [row_tile(columns)] * 2,
        2 * rows * columns * width,
    )


def attend_back_kernel(
    rate_ref, q_ref, sq_ref, k_ref, sk_ref, v_ref, grad_ref, dq_ref, dk_ref, dv_ref, states
):
    rates, query_decay, key_decay, chunk_decay = decays(rate_ref)
    first = head_lanes()
    same = same_head()
    tables = [within_table(rate) for rate in rates]
    flipped = [within_table(rate, True) for rate in rates]
    masks = [jnp.where(first, 1.0, 0.0).astype(BF16), jnp.where(first, 0.0, 1.0).astype(BF16)]
    chunks = q_ref.shape[0] // CHUNK
    state = jnp.zeros((PAIR, PAIR), F32)
    for index in range(chunks):
        rows = pl.ds(index * CHUNK, CHUNK)
        states[index] = state.astype(BF16)
        if index < chunks - 1:
            keys = (k_ref[rows, :].astype(F32) * key_decay).T.astype(BF16)
            state = chunk_decay * state + jnp.where(same, matmul(keys, v_ref[rows, :]), 0.0)
    carry = jnp.zeros((PAIR, PAIR), F32)
    for index in reversed(range(chunks)):
        rows = pl.ds(index * CHUNK, CHUNK)
        q, k, v, grad = q_ref[rows, :], k_ref[rows, :], v_ref[rows, :], grad_ref[rows, :]
        narrow = carry.astype(BF16)
        dq = times_transpose(grad, states[index]) * query_decay
        dk = times_transpose(v, narrow) * key_decay
        dv = matmul(k, narrow) * key_decay
        for mask, table, turned in zip(masks, tables, flipped):
            q_one, grad_one = q * mask, grad * mask
            weights = (times_transpose(k, q_one) * turned).astype(BF16)
            dv = dv + matmul(weights, grad_one)
            dq = dq + matmul((times_transpose(grad_one, v) * table).astype(BF16), k * mask)
            dk = dk + matmul((times_transpose(v, grad_one) * turned).astype(BF16), q_one)
        dq_ref[rows, :] = (dq * sq_ref[rows, :].astype(F32)).astype(BF16)
        dk_ref[rows, :] = (dk * sk_ref[rows, :].astype(F32)).astype(BF16)
        dv_ref[rows, :] = dv.astype(BF16)
        if index > 0:
            turned_q = q.astype(F32).T.astype(BF16)
            decayed = (grad.astype(F32) * query_decay).astype(BF16)
            carry = chunk_decay * carry + jnp.where(same, matmul(turned_q, decayed), 0.0)


def attend_back(half, attended_grad):
    q, sq, k, sk, v, _, _, rates = half
    rows, columns = q.shape
    return call(
        attend_back_kernel,
        (columns // PAIR,),
        (rates, q, sq, k, sk, v, attended_grad),
        [pl.BlockSpec(memory_space=pltpu.SMEM)] + [pair_spec(rows)] * 6,
        [shaped(rows, columns)] * 3,
        [pair_spec(rows)] * 3,
        30 * rows * columns * CHUNK,
        scratch=[pltpu.VMEM((rows // CHUNK, PAIR, PAIR), BF16)],
    )


def glu_parts(hidden, out_grad, wg_ref, wu_ref, wd_ref, columns, turned=False):
    gate_pre = matmul(hidden, wg_ref[:, columns])
    up_pre = matmul(hidden, wu_ref[:, columns])
    if turned:
        glu_grad = matmul(out_grad, wd_ref[:, columns])
    else:
        glu_grad = times_transpose(out_grad, wd_ref[columns, :])
    logistic = jax.nn.sigmoid(gate_pre)
    act = gate_pre * logistic
    glu = (act * up_pre).astype(BF16)
    up_grad = (glu_grad * act).astype(BF16)
    gate_grad = (glu_grad * up_pre * (logistic * (1.0 + gate_pre * (1.0 - logistic)))).astype(BF16)
    return glu, gate_grad, up_grad


def unit_slices(units):
    step = 512
    return [slice(low, min(low + step, units)) for low in range(0, units, step)]


def middle_kernel(
    inputs_ref, live_ref, dy_ref, mixed_a_ref, mixed_b_ref, wo_a_ref, wo_b_ref, gain_ref, wg_ref, wu_ref, wd_ref,
    residual_ref, hidden_ref, glu_ref, gate_grad_ref, up_grad_ref, branch_ref, back_ref,
):
    live = live_ref[...]
    branch = matmul(mixed_a_ref[...], wo_a_ref[...]) + matmul(mixed_b_ref[...], wo_b_ref[...])
    residual = inputs_ref[...].astype(F32) + live * branch
    residual_ref[...] = residual
    scale = lax.rsqrt(row_mean(residual * residual) + EPS)
    hidden = (residual * scale * gain_ref[...].astype(F32)).astype(BF16)
    hidden_ref[...] = hidden
    out_grad = (live * dy_ref[...].astype(F32)).astype(BF16)
    units = wg_ref.shape[1]
    for columns in unit_slices(units):
        glu, gate_grad, up_grad = glu_parts(hidden, out_grad, wg_ref, wu_ref, wd_ref, columns)
        glu_ref[:, columns] = glu
        gate_grad_ref[:, columns] = gate_grad
        up_grad_ref[:, columns] = up_grad
    branch_ref[...] = matmul(glu_ref[...], wd_ref[...])
    back_ref[...] = times_transpose(gate_grad_ref[...], wg_ref[...]) + times_transpose(up_grad_ref[...], wu_ref[...])


def middle(inputs, live, dy, mixed, outs, gain, glus):
    rows, width = inputs.shape
    heads = mixed[0].shape[1]
    units = glus[0].shape[1]
    return call(
        middle_kernel,
        (rows // TILE,),
        (inputs, live, dy, *mixed, *outs, gain, *glus),
        [row_tile(width), row_tile(1), row_tile(width), row_tile(heads), row_tile(heads)]
        + [whole(w) for w in (*outs, gain, *glus)],
        [shaped(rows, width, F32), shaped(rows, width)]
        + [shaped(rows, units)] * 3
        + [shaped(rows, width, F32)] * 2,
        [row_tile(width)] * 2 + [row_tile(units)] * 3 + [row_tile(width)] * 2,
        2 * rows * width * (2 * heads + 6 * units),
    )


def norm_back(grad, normed, scale):
    return scale * (grad - normed * row_mean(grad * normed))


def middle_back_kernel(
    residual_ref, hidden_ref, live_ref, dy_ref, branch_ref, back_ref, gain_ref, wg_ref, wu_ref, wd_ref,
    result_ref, mid_ref, grad_ref, gain_grad_ref, glu_buf, gate_buf, up_buf,
):
    live = live_ref[...]
    dy = dy_ref[...].astype(F32)
    hidden = hidden_ref[...]
    out_grad = (live * dy).astype(BF16)
    for columns in unit_slices(wg_ref.shape[1]):
        glu_buf[:, columns], gate_buf[:, columns], up_buf[:, columns] = glu_parts(
            hidden, out_grad, wg_ref, wu_ref, wd_ref, columns, True
        )
    residual = residual_ref[...]
    branch = branch_ref[...] + times_transpose(glu_buf[...], wd_ref[...])
    result_ref[...] = (residual + live * branch).astype(BF16)
    back = back_ref[...] + times_transpose(gate_buf[...], wg_ref[...]) + times_transpose(up_buf[...], wu_ref[...])
    scale = lax.rsqrt(row_mean(residual * residual) + EPS)
    normed = residual * scale

    @pl.when(pl.program_id(0) == 0)
    def _():
        gain_grad_ref[...] = jnp.zeros_like(gain_grad_ref)

    gain_grad_ref[...] += jnp.sum(back * normed, axis=0, keepdims=True)
    mid = dy + norm_back(back * gain_ref[...].astype(F32), normed, scale)
    mid_ref[...] = mid
    grad_ref[...] = (live * mid).astype(BF16)


def middle_back(residual, hidden, live, dy, branch, back, gain, glus):
    rows, width = hidden.shape
    units = glus[0].shape[1]
    return call(
        middle_back_kernel,
        (rows // TILE,),
        (residual, hidden, live, dy, branch, back, gain, *glus),
        [row_tile(width), row_tile(width), row_tile(1)]
        + [row_tile(width)] * 3
        + [whole(w) for w in (gain, *glus)],
        [shaped(rows, width), shaped(rows, width, F32), shaped(rows, width), shaped(1, width, F32)],
        [row_tile(width)] * 3 + [pl.BlockSpec((1, width), lambda step: (0, 0))],
        2 * rows * width * 6 * units,
        scratch=[pltpu.VMEM((TILE, units), BF16)] * 3,
    )


def first_back_kernel(inputs_ref, mid_ref, gain_ref, *refs):
    grads, weights, (result_ref, gain_grad_ref) = refs[:8], refs[8:16], refs[16:]
    back = times_transpose(grads[0][...], weights[0][...])
    for grad, weight in zip(grads[1:], weights[1:]):
        back = back + times_transpose(grad[...], weight[...])
    wide = inputs_ref[...].astype(F32)
    scale = lax.rsqrt(row_mean(wide * wide) + EPS)
    normed = wide * scale

    @pl.when(pl.program_id(0) == 0)
    def _():
        gain_grad_ref[...] = jnp.zeros_like(gain_grad_ref)

    gain_grad_ref[...] += jnp.sum(back * normed, axis=0, keepdims=True)
    result_ref[...] = (mid_ref[...] + norm_back(back * gain_ref[...].astype(F32), normed, scale)).astype(BF16)


def first_back(inputs, mid, gain, grads, weights):
    rows, width = inputs.shape
    columns = weights[0].shape[1]
    return call(
        first_back_kernel,
        (rows // TILE,),
        (inputs, mid, gain, *grads, *weights),
        [row_tile(width), row_tile(width), whole(gain)]
        + [row_tile(columns)] * 8
        + [whole(w) for w in weights],
        [shaped(rows, width), shaped(1, width, F32)],
        [row_tile(width), pl.BlockSpec((1, width), lambda step: (0, 0))],
        2 * rows * width * columns * 8,
    )


def product_kernel(count, first, came_first, column, plan, left_refs, right_refs, came_ref, out_ref):
    tile = min(TILE, count)
    for low in range(0, count, tile):
        for left, right, start in plan:
            stop = start + right_refs[right].shape[1]
            total = matmul(left_refs[left][first + low : first + low + tile, :], right_refs[right][...])
            if came_ref is not None:
                total = total + came_ref[came_first + low : came_first + low + tile, column + start : column + stop]
            out_ref[low : low + tile, start:stop] = total


def product(lefts, rights, first, count, came=None, came_first=0, column=0):
    distinct = []
    plan = []
    start = 0
    for which, (left, right) in enumerate(zip(lefts, rights)):
        if not any(left is seen for seen in distinct):
            distinct.append(left)
        plan.append(([left is seen for seen in distinct].index(True), which, start))
        start += right.shape[1]
    n_left, n_right = len(distinct), len(rights)

    def body(*refs):
        came_ref = None if came is None else refs[n_left + n_right]
        product_kernel(
            count, first, came_first, column, plan, refs[:n_left], refs[n_left : n_left + n_right], came_ref, refs[-1]
        )

    ins = [*distinct, *rights] + ([] if came is None else [came])
    vmem = pl.BlockSpec(memory_space=pltpu.VMEM)
    return pl.pallas_call(
        body,
        in_specs=[vmem] * len(ins),
        out_specs=vmem,
        out_shape=shaped(count, start, F32),
        cost_estimate=pl.CostEstimate(
            flops=2 * count * lefts[0].shape[1] * start // COST, bytes_accessed=1024, transcendentals=0
        ),
        compiler_params=pltpu.CompilerParams(vmem_limit_bytes=10 * MIB),
    )(*ins)


def products_kernel(left_of, n_left, *refs):
    lefts, rights, out_ref = refs[:n_left], refs[n_left:-1], refs[-1]
    start = 0
    for left, right in zip(left_of, rights):
        stop = start + right.shape[1]
        out_ref[:, start:stop] = matmul(lefts[left][...], right[...])
        start = stop


def products(lefts, left_of, rights):
    rows, depth = lefts[0].shape
    columns = sum(right.shape[1] for right in rights)
    return call(
        functools.partial(products_kernel, left_of, len(lefts)),
        (rows // TILE,),
        (*lefts, *rights),
        [row_tile(depth)] * len(lefts) + [whole(right) for right in rights],
        shaped(rows, columns, F32),
        row_tile(columns),
        2 * rows * depth * columns,
    )


def flip_kernel(array_ref, *refs):
    out_ref = refs[-1]
    for low in range(0, array_ref.shape[1], PAIR):
        values = array_ref[:, low : low + PAIR].astype(F32)
        if len(refs) == 2:
            values = values * refs[0][...]
        out_ref[low : low + PAIR, :] = values.T.astype(BF16)


def flip(array, live=None):
    rows, width = array.shape
    lives = () if live is None else (live,)
    vmem = pl.BlockSpec(memory_space=pltpu.VMEM)
    return pl.pallas_call(
        flip_kernel,
        out_shape=shaped(width, rows),
        in_specs=[vmem] * (1 + len(lives)),
        out_specs=vmem,
        cost_estimate=pl.CostEstimate(flops=1024, bytes_accessed=1024, transcendentals=0),
        compiler_params=pltpu.CompilerParams(vmem_limit_bytes=10 * MIB),
    )(array, *lives)


def turn_kernel(near_first, place_ref, array_ref, *refs):
    out_ref, turned = refs[-2:]
    core, chip = place_ref[0] % 2, place_ref[0] // 2
    part = out_ref.shape[1] // 8
    for step in range(8):
        high, middle_bit, low = step // 4, (step // 2) % 2, step % 2
        across, near, far = (low, high, middle_bit) if near_first else (high, middle_bit, low)
        block = chip ^ (far * 4 + near * 2 + across)
        values = array_ref[:, pl.ds(pl.multiple_of(block * 2 * part, 2 * part), 2 * part)].astype(F32)
        if len(refs) == 3:
            values = values * refs[0][...]
        turned[...] = values.T
        rows = slice(step * part, (step + 1) * part)
        out_ref[0, rows, :] = turned[pl.ds(pl.multiple_of(core * part, part), part), :].astype(BF16)
        out_ref[1, rows, :] = turned[pl.ds(pl.multiple_of((1 - core) * part, part), part), :].astype(BF16)


def turn(array, place, near_first=False, live=None):
    rows, width = array.shape
    lives = () if live is None else (live,)
    vmem = pl.BlockSpec(memory_space=pltpu.VMEM)
    out = pl.pallas_call(
        functools.partial(turn_kernel, near_first),
        out_shape=jax.ShapeDtypeStruct((2, width // 2, rows), BF16),
        in_specs=[pl.BlockSpec(memory_space=pltpu.SMEM)] + [vmem] * (1 + len(lives)),
        out_specs=vmem,
        scratch_shapes=[pltpu.VMEM((width // 8, rows), F32)],
        cost_estimate=pl.CostEstimate(flops=1024, bytes_accessed=1024, transcendentals=0),
        compiler_params=pltpu.CompilerParams(vmem_limit_bytes=10 * MIB),
    )(place, array, *lives)
    return out.reshape(width, rows)


CORE, ACROSS_X, NEAR_Z, FAR_Z = 1, 2, 4, 8


def hold(*trees):
    return lax.optimization_barrier(trees)


def swap_dp(array, bit, size=16):
    return lax.ppermute(array, "dp", [(place, place ^ bit) for place in range(size)])


def swap_tensor(array):
    return lax.ppermute(array, "tensor", [(0, 1), (1, 0)])


def cut_kernel(count, place_ref, *refs):
    out_ref = refs[-1]
    part = refs[0].shape[0]
    for which in range(count):
        out_ref[which * part : (which + 1) * part, :] = refs[which][...].astype(F32)


def cut(weights, place, parts, flips=(0,)):
    rows, columns = weights[0].shape
    part = rows // parts
    count = len(weights) * len(flips)
    specs = [
        pl.BlockSpec((part, columns), lambda step, ref, bits=bits: (ref[0] ^ bits, 0))
        for bits in flips
        for _ in weights
    ]
    return pl.pallas_call(
        functools.partial(cut_kernel, count),
        out_shape=shaped(count * part, columns, F32),
        grid_spec=pltpu.PrefetchScalarGridSpec(
            num_scalar_prefetch=1,
            grid=(1,),
            in_specs=specs,
            out_specs=pl.BlockSpec((count * part, columns), lambda step, ref: (0, 0)),
        ),
        cost_estimate=pl.CostEstimate(flops=1024, bytes_accessed=1024, transcendentals=0),
        compiler_params=pltpu.CompilerParams(vmem_limit_bytes=20 * MIB),
    )(place, *(list(weights) * len(flips)))


def spread_kernel(wide_ref, *outs):
    part = outs[0].shape[0] // 2
    for place in range(2):
        for which, out in enumerate(outs):
            start = (place * len(outs) + which) * part
            out[place * part : (place + 1) * part, :] = wide_ref[start : start + part, :].astype(BF16)


def spread(wide, count):
    rows, columns = wide.shape
    return call(
        spread_kernel,
        (8,),
        (wide,),
        [row_tile(columns, rows // 8)],
        [shaped(rows // count, columns)] * count,
        [row_tile(columns, rows // 8 // count)] * count,
        1024,
    )


def place_kernel(count, place_ref, *refs):
    pieces, outs = refs[:8], refs[8:]
    place = place_ref[0]
    part = outs[0].shape[0] // 8
    for index in range(8):
        target = place ^ index
        for which in range(count):
            outs[which][pl.ds(pl.multiple_of(target * part, part), part), :] = pieces[index][
                which * part : (which + 1) * part, :
            ].astype(BF16)


def put(pieces, count, place):
    height, columns = pieces[0].shape
    rows = 8 * height // count
    once = dict(pipeline_mode=pl.Buffered(1))
    return pl.pallas_call(
        functools.partial(place_kernel, count),
        out_shape=[shaped(rows, columns)] * count,
        grid_spec=pltpu.PrefetchScalarGridSpec(
            num_scalar_prefetch=1,
            grid=(1,),
            in_specs=[pl.BlockSpec((height, columns), lambda step, ref: (0, 0), **once)] * 8,
            out_specs=[pl.BlockSpec((rows, columns), lambda step, ref: (0, 0), **once)] * count,
        ),
        cost_estimate=pl.CostEstimate(flops=1024, bytes_accessed=1024, transcendentals=0),
        compiler_params=pltpu.CompilerParams(vmem_limit_bytes=20 * MIB),
    )(place, *pieces)


def cast_kernel(wide_ref, out_ref):
    out_ref[...] = wide_ref[...].astype(BF16)


def cast_weight(wide):
    rows, columns = wide.shape
    spec = pl.BlockSpec((rows // 8, columns), lambda row: (row, 0))
    return pl.pallas_call(
        cast_kernel, grid=(8,), out_shape=jax.ShapeDtypeStruct(wide.shape, BF16), in_specs=[spec], out_specs=spec
    )(wide)


def relative_rows(array, dp_place, order):
    blocks = array.reshape(2, 2, 2, 2, array.shape[0] // 16, array.shape[1])
    for axis, bit in enumerate((FAR_Z, NEAR_Z, ACROSS_X, CORE)):
        blocks = jnp.where((dp_place & bit) > 0, jnp.flip(blocks, axis), blocks)
    axes = {FAR_Z: 0, NEAR_Z: 1, ACROSS_X: 2, CORE: 3}
    return blocks.transpose([axes[bit] for bit in order] + [4, 5]).reshape(array.shape)


ORDER_X = (CORE, ACROSS_X, NEAR_Z, FAR_Z)
ORDER_Z = (CORE, NEAR_Z, FAR_Z, ACROSS_X)


class Scatter:
    def __init__(self, lefts, rights, order, came, column):
        self.order, self.stage = order, 1
        part = lefts[0].shape[0] // 4
        self.send = product(lefts, rights, part, part, came, part, column)
        self.kept = product(lefts, rights, 0, part, came, 0, column)

    def go(self):
        self.came = swap_dp(self.send, self.order[self.stage])
        self.stage += 1

    def step(self):
        half = self.kept.shape[0] // 2
        self.send = self.kept[half:] + self.came[half:]
        self.kept = self.kept[:half] + self.came[:half]
        self.go()

    def total(self):
        return self.kept + self.came


def scatter_vector(vector, dp_place):
    kept = relative_rows(vector, dp_place, ORDER_X)
    for bit in ORDER_X:
        half = kept.shape[0] // 2
        kept = kept[:half] + swap_dp(kept[half:], bit)
    return kept


def rates_of(side, local_heads):
    head_ids = jnp.arange(local_heads)
    return tuple(
        jnp.exp2(-8.0 * ((which * local_heads + head_ids).astype(F32) + 1.0) / HEADS)
        for which in (side, 1 - side)
    )


def forward_half(hidden, live, weights, rates):
    parts = project(hidden, live, weights)
    q, sq, k, sk, v, gate = parts
    attended, mixed = attend(q, k, v, gate, rates)
    return (*parts, attended, rates), mixed


def shards_plain(
    inputs, lengths, gain_attn, w_query, w_key, w_value, w_gate_attn, w_out, gain_ffn, w_gate, w_up, w_down, cotangent
):
    own = (w_query, w_key, w_value, w_gate_attn, w_out, w_gate, w_up, w_down)
    others = [cast_weight(swap_tensor(weight.astype(F32))) for weight in own]
    rates = rates_of(lax.axis_index("tensor"), w_query.shape[1] // HEAD_DIM)
    positions = jnp.arange(inputs.shape[0], dtype=jnp.int32)
    live = (positions < lengths[0]).astype(F32)[:, None]
    gain_one, gain_two = gain_attn.reshape(1, -1), gain_ffn.reshape(1, -1)
    out_grad = (live * cotangent.astype(F32)).astype(BF16)
    hidden_one = first_norm(inputs, gain_one)
    half_a, mixed_a = forward_half(hidden_one, live, own[:4], rates[0])
    half_b, mixed_b = forward_half(hidden_one, live, others[:4], rates[1])
    residual, hidden_two, glu, gate_grad, up_grad, branch, back = middle(
        inputs, live, cotangent, (mixed_a, mixed_b), (w_out, others[4]), gain_two, own[5:]
    )
    result, mid_grad, attn_out_grad, gain_two_grad = middle_back(
        residual, hidden_two, live, cotangent, branch, back, gain_two, (others[5], others[6], others[7].T)
    )
    open_a, gate_a = open_back(half_a, attn_out_grad, w_out)
    open_b, gate_b = open_back(half_b, attn_out_grad, others[4])
    back_a = (*attend_back(half_a, open_a), gate_a)
    back_b = (*attend_back(half_b, open_b), gate_b)
    input_grad, gain_one_grad = first_back(
        inputs, mid_grad, gain_one, (*back_a, *back_b), (*own[:4], *others[:4])
    )
    pairs = [(hidden_one, grad) for grad in back_a]
    pairs += [(attn_out_grad, mixed_a), (hidden_two, gate_grad), (hidden_two, up_grad), (out_grad, glu)]
    sums = [
        lax.psum_scatter(matmul(left.T, right), "dp", scatter_dimension=0, tiled=True) for left, right in pairs
    ]
    gains = [lax.psum_scatter(grad[0], "dp", scatter_dimension=0, tiled=True) for grad in (gain_one_grad, gain_two_grad)]
    return (result, input_grad, gains[0], *sums[:4], sums[4].T, gains[1], sums[5], sums[6], sums[7].T)


def shards_here(
    inputs, lengths, gain_attn, w_query, w_key, w_value, w_gate_attn, w_out, gain_ffn, w_gate, w_up, w_down, cotangent
):
    seq_rows = inputs.shape[0]
    side = lax.axis_index("tensor")
    dp_place = lax.axis_index("dp")
    place = (dp_place % 8).reshape(1)
    rates = rates_of(side, w_query.shape[1] // HEAD_DIM)
    positions = jnp.arange(seq_rows, dtype=jnp.int32)
    live = (positions < lengths[0]).astype(F32)[:, None]
    gain_one = gain_attn.reshape(1, -1)
    gain_two = gain_ffn.reshape(1, -1)

    proj = (w_query, w_key, w_value, w_gate_attn)
    whole_place = dp_place.reshape(1)
    y1 = swap_tensor(cut(proj, place, 8))
    features = w_down.shape[1] // 16
    down_piece = lax.dynamic_slice_in_dim(w_down, dp_place * features, features, 1).T
    glu_cut = jnp.concatenate([cut((w_gate, w_up), whole_place, 16), down_piece.astype(F32)], axis=0)
    y2_cut, out_cut = cut(proj, place ^ 6, 8), cut((w_out,), place, 8, (0, 6))
    hidden_one = first_norm(inputs, gain_one)
    parts = project(hidden_one, live, proj)

    y1, parts, glu_cut, out = hold(y1, parts, glu_cut, out_cut)
    out = swap_tensor(out)
    x1, z1, y1c = swap_dp(y1, ACROSS_X), swap_dp(y1, NEAR_Z), swap_dp(y1, CORE)
    glu_cut = swap_tensor(glu_cut)
    q, sq, k, sk, v, gate = parts
    attended, mixed_a = attend(q, k, v, gate, rates[0])
    half_a = (*parts, attended, rates[0])
    dy_t = flip(cotangent, live)

    x1, z1, y1c, glu_cut, mixed_a, dy_t, hidden_one, y2, out = hold(
        x1, z1, y1c, glu_cut, mixed_a, dy_t, hidden_one, y2_cut, out
    )
    part = out.shape[0] // 2
    ox, oz = swap_dp(out[:part], ACROSS_X), swap_dp(out[:part], NEAR_Z)
    glu_wide = lax.all_gather(glu_cut, "dp", axis=0, tiled=True)
    y2 = swap_tensor(y2)
    x1c, z1c = swap_dp(x1, CORE), swap_dp(z1, CORE)
    hidden_one_t = turn(hidden_one, whole_place)
    hidden_one_tz = turn(hidden_one, whole_place, near_first=True)

    y2, x1c, z1c, ox, oz, hidden_one_t, hidden_one_tz = hold(y2, x1c, z1c, ox, oz, hidden_one_t, hidden_one_tz)
    y2c = swap_dp(y2, CORE)
    out_c, out_xz = swap_dp(out, CORE), swap_dp(jnp.concatenate([ox, oz], axis=0), CORE)
    proj_b = put((y1, y1c, x1, x1c, z1, z1c, y2, y2c), 4, place)
    parts = project(hidden_one, live, proj_b)

    parts, out_c, out_xz = hold(parts, out_c, out_xz)
    (w_out_b,) = put(
        (out[:part], out_c[:part], ox, out_xz[:part], oz, out_xz[part:], out[part:], out_c[part:]), 1, place
    )
    q, sq, k, sk, v, gate = parts
    attended, mixed_b = attend(q, k, v, gate, rates[1])
    half_b = (*parts, attended, rates[1])

    residual, hidden_two, glu, gate_grad, up_grad, branch, back = middle(
        inputs, live, cotangent, (mixed_a, mixed_b), (w_out, others[4]), gain_two, own[5:]
    )
    result, mid_grad, attn_out_grad, gain_two_grad = middle_back(
        residual, hidden_two, live, cotangent, branch, back, gain_two, (others[5], others[6], others[7].T)
    )
    open_a, gate_a = open_back(half_a, attn_out_grad, w_out)
    open_b, gate_b = open_back(half_b, attn_out_grad, others[4])
    back_a = (*attend_back(half_a, open_a), gate_a)
    back_b = (*attend_back(half_b, open_b), gate_b)
    input_grad, gain_one_grad = first_back(
        inputs, mid_grad, gain_one, (*back_a, *back_b), (*own[:4], *others[:4])
    )
    pairs = [(hidden_one, grad) for grad in back_a]
    pairs += [(attn_out_grad, mixed_a), (hidden_two, gate_grad), (hidden_two, up_grad), (out_grad, glu)]
    sums = [
        lax.psum_scatter(matmul(left.T, right), "dp", scatter_dimension=0, tiled=True) for left, right in pairs
    ]
    gains = [lax.psum_scatter(grad[0], "dp", scatter_dimension=0, tiled=True) for grad in (gain_one_grad, gain_two_grad)]
    return (result, input_grad, gains[0], *sums[:4], sums[4].T, gains[1], sums[5], sums[6], sums[7].T)


def shards_here(
    inputs, lengths, gain_attn, w_query, w_key, w_value, w_gate_attn, w_out, gain_ffn, w_gate, w_up, w_down, cotangent
):
    seq_rows = inputs.shape[0]
    side = lax.axis_index("tensor")
    dp_place = lax.axis_index("dp")
    place = (dp_place % 8).reshape(1)
    rates = rates_of(side, w_query.shape[1] // HEAD_DIM)
    positions = jnp.arange(seq_rows, dtype=jnp.int32)
    live = (positions < lengths[0]).astype(F32)[:, None]
    gain_one = gain_attn.reshape(1, -1)
    gain_two = gain_ffn.reshape(1, -1)

    proj = (w_query, w_key, w_value, w_gate_attn)
    whole_place = dp_place.reshape(1)
    y1 = swap_tensor(cut(proj, place, 8))
    features = w_down.shape[1] // 16
    down_piece = lax.dynamic_slice_in_dim(w_down, dp_place * features, features, 1).T
    glu_cut = jnp.concatenate([cut((w_gate, w_up), whole_place, 16), down_piece.astype(F32)], axis=0)
    y2_cut, out_cut = cut(proj, place ^ 6, 8), cut((w_out,), place, 8, (0, 6))
    hidden_one = first_norm(inputs, gain_one)
    parts = project(hidden_one, live, proj)

    y1, parts, glu_cut, out = hold(y1, parts, glu_cut, out_cut)
    out = swap_tensor(out)
    x1, z1, y1c = swap_dp(y1, ACROSS_X), swap_dp(y1, NEAR_Z), swap_dp(y1, CORE)
    glu_cut = swap_tensor(glu_cut)
    q, sq, k, sk, v, gate = parts
    attended, mixed_a = attend(q, k, v, gate, rates[0])
    half_a = (*parts, attended, rates[0])
    dy_t = flip(cotangent, live)

    x1, z1, y1c, glu_cut, mixed_a, dy_t, hidden_one, y2, out = hold(
        x1, z1, y1c, glu_cut, mixed_a, dy_t, hidden_one, y2_cut, out
    )
    part = out.shape[0] // 2
    ox, oz = swap_dp(out[:part], ACROSS_X), swap_dp(out[:part], NEAR_Z)
    glu_wide = lax.all_gather(glu_cut, "dp", axis=0, tiled=True)
    y2 = swap_tensor(y2)
    x1c, z1c = swap_dp(x1, CORE), swap_dp(z1, CORE)
    hidden_one_t = turn(hidden_one, whole_place)
    hidden_one_tz = turn(hidden_one, whole_place, near_first=True)

    y2, x1c, z1c, ox, oz, hidden_one_t, hidden_one_tz = hold(y2, x1c, z1c, ox, oz, hidden_one_t, hidden_one_tz)
    y2c = swap_dp(y2, CORE)
    out_c, out_xz = swap_dp(out, CORE), swap_dp(jnp.concatenate([ox, oz], axis=0), CORE)
    proj_b = put((y1, y1c, x1, x1c, z1, z1c, y2, y2c), 4, place)
    parts = project(hidden_one, live, proj_b)

    parts, out_c, out_xz = hold(parts, out_c, out_xz)
    (w_out_b,) = put(
        (out[:part], out_c[:part], ox, out_xz[:part], oz, out_xz[part:], out[part:], out_c[part:]), 1, place
    )
    q, sq, k, sk, v, gate = parts
    attended, mixed_b = attend(q, k, v, gate, rates[1])
    half_b = (*parts, attended, rates[1])

    mixed_b, out_xz = hold(mixed_b, out_xz)
    (w_out_b,) = put(
        (out[:part], out_c[:part], ox, out_xz[:part], oz, out_xz[part:], out[part:], out_c[part:]), 1, place
    )
    residual, hidden_two, glu, gate_grad, up_grad, branch, back = middle(
        inputs, live, cotangent, (mixed_a, mixed_b), (w_out, w_out_b), gain_two, (w_gate, w_up, w_down)
    )
    wide = products((dy_t, flip(hidden_two)), (0, 1, 1), (glu, gate_grad, up_grad))

    residual, wide = hold(residual, wide)
    units = glu.shape[1]
    ffn_sums = lax.psum_scatter(wide, "dp", scatter_dimension=0, tiled=True)
    result, mid_grad, attn_out_grad, gain_two_grad = middle_back(
        residual, hidden_two, live, cotangent, branch, back, gain_two, spread(glu_wide, 3)
    )

    half = dy_t.shape[0] // 2
    open_a, gate_a = open_back(half_a, attn_out_grad, w_out)
    attn_out_grad_t = turn(attn_out_grad, whole_place, near_first=True)
    lefts, rights = (attn_out_grad_t, hidden_one_tz), (mixed_a, gate_a)
    came = swap_dp(product(lefts, rights, half, half), CORE)

    open_a, came, attn_out_grad = hold(open_a, came, attn_out_grad)
    second = Scatter(lefts, rights, ORDER_Z, came, 0)
    second.go()
    own = attend_back(half_a, open_a)

    own, attn_out_grad = hold(own, attn_out_grad)
    lefts = (hidden_one_t,) * 3
    came = swap_dp(product(lefts, own, half, half), CORE)
    open_b, gate_b = open_back(half_b, attn_out_grad, w_out_b)

    open_b, came = hold(open_b, came)
    first = Scatter(lefts, own, ORDER_X, came, 0)
    first.go()
    other = attend_back(half_b, open_b)

    own, other = (*own, gate_a), (*other, gate_b)
    input_grad, gain_one_grad = first_back(inputs, mid_grad, gain_one, (*own, *other), (*proj, *proj_b))

    input_grad, first.came, second.came, gain_one_grad = hold(input_grad, first.came, second.came, gain_one_grad)
    first.step()
    second.step()
    gains = scatter_vector(jnp.concatenate([gain_one_grad, gain_two_grad], axis=0).T, dp_place)
    first.came, second.came, gains = hold(first.came, second.came, gains)
    first.step()
    second.step()
    first_sum, second_sum = first.total(), second.total()
    first_sum, second_sum, ffn_sums = hold(first_sum, second_sum, ffn_sums)
    width = w_query.shape[1]
    return (
        result,
        input_grad,
        gains[:, 0],
        first_sum[:, :width],
        first_sum[:, width : 2 * width],
        first_sum[:, 2 * width :],
        second_sum[:, width:],
        second_sum[:, :width].T,
        gains[:, 1],
        ffn_sums[:, units : 2 * units],
        ffn_sums[:, 2 * units :],
        ffn_sums[:, :units].T,
    )


def solution(mesh):
    placed = (
        P("dp", None),
        P("dp"),
        P(),
        P(None, "tensor"),
        P(None, "tensor"),
        P(None, "tensor"),
        P(None, "tensor"),
        P("tensor", None),
        P(),
        P(None, "tensor"),
        P(None, "tensor"),
        P("tensor", None),
        P("dp", None),
    )
    return jax.shard_map(
        shards_here if mesh.shape["dp"] == 16 else shards_plain,
        mesh=mesh,
        in_specs=placed,
        out_specs=(
            P("dp", None),
            P("dp", None),
            P("dp"),
            P("dp", "tensor"),
            P("dp", "tensor"),
            P("dp", "tensor"),
            P("dp", "tensor"),
            P("tensor", "dp"),
            P("dp"),
            P("dp", "tensor"),
            P("dp", "tensor"),
            P("tensor", "dp"),
        ),
        check_vma=False,
    )
```

```python
import functools

import jax
import jax.numpy as jnp
from jax import lax
from jax.experimental import pallas as pl
from jax.experimental.pallas import tpu as pltpu
from jax.sharding import PartitionSpec as P

HEADS = 16
HEAD_DIM = 64
BLOCK = 512
EPS = 1e-06
HIGHEST = lax.Precision.HIGHEST
F32 = jnp.float32
BF16 = jnp.bfloat16


def matmul(left, right):
    return jnp.dot(left, right, preferred_element_type=F32)


def times_transpose(left, right):
    return lax.dot_general(left, right, (((1,), (1,)), ((), ())), preferred_element_type=F32)


def row_mean(array):
    return jnp.mean(array, axis=1, keepdims=True)


MIB = 2**20
COST = 1000
TILE = 256
CHUNK = 256
PAIR = 2 * HEAD_DIM


def whole(array):
    return pl.BlockSpec(array.shape, lambda *_: (0,) * array.ndim, pipeline_mode=pl.Buffered(1))


def row_tile(columns, rows=TILE):
    return pl.BlockSpec((rows, columns), lambda step: (step, 0))


def call(body, grid, ins, in_specs, outs, out_specs, flops, scratch=(), limit=34):
    return pl.pallas_call(
        body,
        grid=grid,
        in_specs=in_specs,
        out_specs=out_specs,
        out_shape=outs,
        scratch_shapes=scratch,
        cost_estimate=pl.CostEstimate(flops=int(flops) // COST, bytes_accessed=1024, transcendentals=0),
        compiler_params=pltpu.CompilerParams(vmem_limit_bytes=limit * MIB),
    )(*ins)


def shaped(rows, columns, kind=BF16):
    return jax.ShapeDtypeStruct((rows, columns), kind)


def norm_kernel(inputs_ref, gain_ref, hidden_ref):
    wide = inputs_ref[...].astype(F32)
    scale = lax.rsqrt(row_mean(wide * wide) + EPS)
    hidden_ref[...] = (wide * scale * gain_ref[...].astype(F32)).astype(BF16)


def first_norm(inputs, gain):
    rows, width = inputs.shape
    return call(
        norm_kernel,
        (rows // TILE,),
        (inputs, gain),
        [row_tile(width), whole(gain)],
        shaped(rows, width),
        row_tile(width),
        rows * width * 8,
    )


def project_kernel(hidden_ref, live_ref, wq_ref, wk_ref, wv_ref, wg_ref, q_ref, sq_ref, k_ref, sk_ref, v_ref, gate_ref):
    hidden = hidden_ref[...]
    live = live_ref[...]

    def activate(value):
        small = jnp.exp(-jnp.abs(value))
        share = 1.0 / (1.0 + small)
        return jnp.maximum(value, 0.0) + jnp.log1p(small), jnp.where(value >= 0.0, share, small * share)

    positive, slope = activate(matmul(hidden, wq_ref[...]))
    q_ref[...] = positive.astype(BF16)
    sq_ref[...] = slope.astype(BF16)
    positive, slope = activate(matmul(hidden, wk_ref[...]))
    k_ref[...] = (positive * live).astype(BF16)
    sk_ref[...] = (slope * live).astype(BF16)
    v_ref[...] = matmul(hidden, wv_ref[...]).astype(BF16)
    gate_ref[...] = jax.nn.sigmoid(matmul(hidden, wg_ref[...]))


def project(hidden, live, weights):
    rows, width = hidden.shape
    columns = weights[0].shape[1]
    narrow = shaped(rows, columns)
    return call(
        project_kernel,
        (rows // TILE,),
        (hidden, live, *weights),
        [row_tile(width), row_tile(1)] + [whole(w) for w in weights],
        [narrow] * 5 + [shaped(rows, columns, F32)],
        [row_tile(columns)] * 6,
        8 * rows * width * columns,
    )


def head_lanes():
    return lax.broadcasted_iota(jnp.int32, (1, PAIR), 1) < HEAD_DIM


def same_head():
    rows = lax.broadcasted_iota(jnp.int32, (PAIR, PAIR), 0) < HEAD_DIM
    columns = lax.broadcasted_iota(jnp.int32, (PAIR, PAIR), 1) < HEAD_DIM
    return rows == columns


def head_mean(array, ones):
    high = array.astype(BF16)
    low = (array - high.astype(F32)).astype(BF16)
    return (matmul(high, ones) + matmul(low, ones)) * (1.0 / HEAD_DIM)


def decays(rate_ref):
    pair = pl.program_id(0)
    rates = (rate_ref[2 * pair], rate_ref[2 * pair + 1])
    lane_rate = jnp.where(head_lanes(), rates[0], rates[1])
    place = lax.broadcasted_iota(jnp.int32, (CHUNK, 1), 0).astype(F32)
    query_decay = jnp.exp(-lane_rate * (place + 1.0))
    key_decay = jnp.exp(-lane_rate * (CHUNK - 1.0 - place))
    chunk_decay = jnp.exp(-lane_rate * CHUNK)
    return rates, query_decay, key_decay, chunk_decay


def within_table(rate, flipped=False):
    rows = lax.broadcasted_iota(jnp.int32, (CHUNK, CHUNK), 0)
    columns = lax.broadcasted_iota(jnp.int32, (CHUNK, CHUNK), 1)
    spread = columns - rows if flipped else rows - columns
    kept = spread >= 0
    return jnp.where(kept, jnp.exp(-rate * jnp.where(kept, spread, 0).astype(F32)), 0.0)


def attend_kernel(rate_ref, q_ref, k_ref, v_ref, gate_ref, attended_ref, mixed_ref):
    rates, query_decay, key_decay, chunk_decay = decays(rate_ref)
    first = head_lanes()
    same = same_head()
    ones = jnp.where(same, 1.0, 0.0).astype(BF16)
    tables = [within_table(rate) for rate in rates]
    masks = [jnp.where(first, 1.0, 0.0).astype(BF16), jnp.where(first, 0.0, 1.0).astype(BF16)]
    state = jnp.zeros((PAIR, PAIR), F32)
    for index in range(q_ref.shape[0] // CHUNK):
        rows = pl.ds(index * CHUNK, CHUNK)
        q, k, v = q_ref[rows, :], k_ref[rows, :], v_ref[rows, :]
        attended = matmul(q, state.astype(BF16)) * query_decay
        for mask, table in zip(masks, tables):
            weights = (times_transpose(q * mask, k) * table).astype(BF16)
            attended = attended + matmul(weights, v * mask)
        keys = (k.astype(F32) * key_decay).T.astype(BF16)
        state = chunk_decay * state + jnp.where(same, matmul(keys, v), 0.0)
        scale = lax.rsqrt(head_mean(attended * attended, ones) + EPS)
        attended_ref[rows, :] = attended
        mixed_ref[rows, :] = (attended * scale * gate_ref[rows, :]).astype(BF16)


def pair_spec(rows):
    return pl.BlockSpec((rows, PAIR), lambda pair: (0, pair))


def attend(q, k, v, gate, rates):
    rows, columns = q.shape
    return call(
        attend_kernel,
        (columns // PAIR,),
        (rates, q, k, v, gate),
        [pl.BlockSpec(memory_space=pltpu.SMEM)] + [pair_spec(rows)] * 4,
        [shaped(rows, columns, F32), shaped(rows, columns)],
        [pair_spec(rows)] * 2,
        12 * rows * columns * CHUNK,
    )


def open_back_kernel(gate_ref, attended_ref, grad_ref, wo_ref, out_grad_ref, dg_ref):
    ones = jnp.where(same_head(), 1.0, 0.0).astype(BF16)
    wide = times_transpose(grad_ref[...], wo_ref[...])
    for low in range(0, wide.shape[1], PAIR):
        lanes = slice(low, low + PAIR)
        mixed_grad, attended, gate = wide[:, lanes], attended_ref[:, lanes], gate_ref[:, lanes]
        scale = lax.rsqrt(head_mean(attended * attended, ones) + EPS)
        normed = attended * scale
        dg_ref[:, lanes] = (mixed_grad * normed * gate * (1.0 - gate)).astype(BF16)
        normed_grad = mixed_grad * gate
        out_grad_ref[:, lanes] = (scale * (normed_grad - normed * head_mean(normed_grad * normed, ones))).astype(BF16)


def open_back(half, out_grad, w_out):
    gate, attended = half[5:7]
    rows, columns = gate.shape
    width = out_grad.shape[1]
    return call(
        open_back_kernel,
        (rows // TILE,),
        (gate, attended, out_grad, w_out),
        [row_tile(columns), row_tile(columns), row_tile(width), whole(w_out)],
        [shaped(rows, columns)] * 2,
        [row_tile(columns)] * 2,
        2 * rows * columns * width,
    )


def attend_back_kernel(
    rate_ref, q_ref, sq_ref, k_ref, sk_ref, v_ref, grad_ref, dq_ref, dk_ref, dv_ref, states
):
    rates, query_decay, key_decay, chunk_decay = decays(rate_ref)
    first = head_lanes()
    same = same_head()
    tables = [within_table(rate) for rate in rates]
    flipped = [within_table(rate, True) for rate in rates]
    masks = [jnp.where(first, 1.0, 0.0).astype(BF16), jnp.where(first, 0.0, 1.0).astype(BF16)]
    chunks = q_ref.shape[0] // CHUNK
    state = jnp.zeros((PAIR, PAIR), F32)
    for index in range(chunks):
        rows = pl.ds(index * CHUNK, CHUNK)
        states[index] = state.astype(BF16)
        if index < chunks - 1:
            keys = (k_ref[rows, :].astype(F32) * key_decay).T.astype(BF16)
            state = chunk_decay * state + jnp.where(same, matmul(keys, v_ref[rows, :]), 0.0)
    carry = jnp.zeros((PAIR, PAIR), F32)
    for index in reversed(range(chunks)):
        rows = pl.ds(index * CHUNK, CHUNK)
        q, k, v, grad = q_ref[rows, :], k_ref[rows, :], v_ref[rows, :], grad_ref[rows, :]
        narrow = carry.astype(BF16)
        dq = times_transpose(grad, states[index]) * query_decay
        dk = times_transpose(v, narrow) * key_decay
        dv = matmul(k, narrow) * key_decay
        for mask, table, turned in zip(masks, tables, flipped):
            q_one, grad_one = q * mask, grad * mask
            weights = (times_transpose(k, q_one) * turned).astype(BF16)
            dv = dv + matmul(weights, grad_one)
            dq = dq + matmul((times_transpose(grad_one, v) * table).astype(BF16), k * mask)
            dk = dk + matmul((times_transpose(v, grad_one) * turned).astype(BF16), q_one)
        dq_ref[rows, :] = (dq * sq_ref[rows, :].astype(F32)).astype(BF16)
        dk_ref[rows, :] = (dk * sk_ref[rows, :].astype(F32)).astype(BF16)
        dv_ref[rows, :] = dv.astype(BF16)
        if index > 0:
            turned_q = q.astype(F32).T.astype(BF16)
            decayed = (grad.astype(F32) * query_decay).astype(BF16)
            carry = chunk_decay * carry + jnp.where(same, matmul(turned_q, decayed), 0.0)


def attend_back(half, attended_grad):
    q, sq, k, sk, v, _, _, rates = half
    rows, columns = q.shape
    return call(
        attend_back_kernel,
        (columns // PAIR,),
        (rates, q, sq, k, sk, v, attended_grad),
        [pl.BlockSpec(memory_space=pltpu.SMEM)] + [pair_spec(rows)] * 6,
        [shaped(rows, columns)] * 3,
        [pair_spec(rows)] * 3,
        30 * rows * columns * CHUNK,
        scratch=[pltpu.VMEM((rows // CHUNK, PAIR, PAIR), BF16)],
    )


def glu_parts(hidden, out_grad, wg_ref, wu_ref, wd_ref, columns, turned=False):
    gate_pre = matmul(hidden, wg_ref[:, columns])
    up_pre = matmul(hidden, wu_ref[:, columns])
    if turned:
        glu_grad = matmul(out_grad, wd_ref[:, columns])
    else:
        glu_grad = times_transpose(out_grad, wd_ref[columns, :])
    logistic = jax.nn.sigmoid(gate_pre)
    act = gate_pre * logistic
    glu = (act * up_pre).astype(BF16)
    up_grad = (glu_grad * act).astype(BF16)
    gate_grad = (glu_grad * up_pre * (logistic * (1.0 + gate_pre * (1.0 - logistic)))).astype(BF16)
    return glu, gate_grad, up_grad


def unit_slices(units):
    step = 512
    return [slice(low, min(low + step, units)) for low in range(0, units, step)]


def middle_kernel(
    inputs_ref, live_ref, dy_ref, mixed_a_ref, mixed_b_ref, wo_a_ref, wo_b_ref, gain_ref, wg_ref, wu_ref, wd_ref,
    residual_ref, hidden_ref, glu_ref, gate_grad_ref, up_grad_ref, branch_ref, back_ref,
):
    live = live_ref[...]
    branch = matmul(mixed_a_ref[...], wo_a_ref[...]) + matmul(mixed_b_ref[...], wo_b_ref[...])
    residual = inputs_ref[...].astype(F32) + live * branch
    residual_ref[...] = residual
    scale = lax.rsqrt(row_mean(residual * residual) + EPS)
    hidden = (residual * scale * gain_ref[...].astype(F32)).astype(BF16)
    hidden_ref[...] = hidden
    out_grad = (live * dy_ref[...].astype(F32)).astype(BF16)
    units = wg_ref.shape[1]
    for columns in unit_slices(units):
        glu, gate_grad, up_grad = glu_parts(hidden, out_grad, wg_ref, wu_ref, wd_ref, columns)
        glu_ref[:, columns] = glu
        gate_grad_ref[:, columns] = gate_grad
        up_grad_ref[:, columns] = up_grad
    branch_ref[...] = matmul(glu_ref[...], wd_ref[...])
    back_ref[...] = times_transpose(gate_grad_ref[...], wg_ref[...]) + times_transpose(up_grad_ref[...], wu_ref[...])


def middle(inputs, live, dy, mixed, outs, gain, glus):
    rows, width = inputs.shape
    heads = mixed[0].shape[1]
    units = glus[0].shape[1]
    return call(
        middle_kernel,
        (rows // TILE,),
        (inputs, live, dy, *mixed, *outs, gain, *glus),
        [row_tile(width), row_tile(1), row_tile(width), row_tile(heads), row_tile(heads)]
        + [whole(w) for w in (*outs, gain, *glus)],
        [shaped(rows, width, F32), shaped(rows, width)]
        + [shaped(rows, units)] * 3
        + [shaped(rows, width, F32)] * 2,
        [row_tile(width)] * 2 + [row_tile(units)] * 3 + [row_tile(width)] * 2,
        2 * rows * width * (2 * heads + 6 * units),
    )


def norm_back(grad, normed, scale):
    return scale * (grad - normed * row_mean(grad * normed))


def middle_back_kernel(
    residual_ref, hidden_ref, live_ref, dy_ref, branch_ref, back_ref, gain_ref, wg_ref, wu_ref, wd_ref,
    result_ref, mid_ref, grad_ref, gain_grad_ref, glu_buf, gate_buf, up_buf,
):
    live = live_ref[...]
    dy = dy_ref[...].astype(F32)
    hidden = hidden_ref[...]
    out_grad = (live * dy).astype(BF16)
    for columns in unit_slices(wg_ref.shape[1]):
        glu_buf[:, columns], gate_buf[:, columns], up_buf[:, columns] = glu_parts(
            hidden, out_grad, wg_ref, wu_ref, wd_ref, columns, True
        )
    residual = residual_ref[...]
    branch = branch_ref[...] + times_transpose(glu_buf[...], wd_ref[...])
    result_ref[...] = (residual + live * branch).astype(BF16)
    back = back_ref[...] + times_transpose(gate_buf[...], wg_ref[...]) + times_transpose(up_buf[...], wu_ref[...])
    scale = lax.rsqrt(row_mean(residual * residual) + EPS)
    normed = residual * scale

    @pl.when(pl.program_id(0) == 0)
    def _():
        gain_grad_ref[...] = jnp.zeros_like(gain_grad_ref)

    gain_grad_ref[...] += jnp.sum(back * normed, axis=0, keepdims=True)
    mid = dy + norm_back(back * gain_ref[...].astype(F32), normed, scale)
    mid_ref[...] = mid
    grad_ref[...] = (live * mid).astype(BF16)


def middle_back(residual, hidden, live, dy, branch, back, gain, glus):
    rows, width = hidden.shape
    units = glus[0].shape[1]
    return call(
        middle_back_kernel,
        (rows // TILE,),
        (residual, hidden, live, dy, branch, back, gain, *glus),
        [row_tile(width), row_tile(width), row_tile(1)]
        + [row_tile(width)] * 3
        + [whole(w) for w in (gain, *glus)],
        [shaped(rows, width), shaped(rows, width, F32), shaped(rows, width), shaped(1, width, F32)],
        [row_tile(width)] * 3 + [pl.BlockSpec((1, width), lambda step: (0, 0))],
        2 * rows * width * 6 * units,
        scratch=[pltpu.VMEM((TILE, units), BF16)] * 3,
    )


def first_back_kernel(inputs_ref, mid_ref, gain_ref, *refs):
    grads, weights, (result_ref, gain_grad_ref) = refs[:8], refs[8:16], refs[16:]
    back = times_transpose(grads[0][...], weights[0][...])
    for grad, weight in zip(grads[1:], weights[1:]):
        back = back + times_transpose(grad[...], weight[...])
    wide = inputs_ref[...].astype(F32)
    scale = lax.rsqrt(row_mean(wide * wide) + EPS)
    normed = wide * scale

    @pl.when(pl.program_id(0) == 0)
    def _():
        gain_grad_ref[...] = jnp.zeros_like(gain_grad_ref)

    gain_grad_ref[...] += jnp.sum(back * normed, axis=0, keepdims=True)
    result_ref[...] = (mid_ref[...] + norm_back(back * gain_ref[...].astype(F32), normed, scale)).astype(BF16)


def first_back(inputs, mid, gain, grads, weights):
    rows, width = inputs.shape
    columns = weights[0].shape[1]
    return call(
        first_back_kernel,
        (rows // TILE,),
        (inputs, mid, gain, *grads, *weights),
        [row_tile(width), row_tile(width), whole(gain)]
        + [row_tile(columns)] * 8
        + [whole(w) for w in weights],
        [shaped(rows, width), shaped(1, width, F32)],
        [row_tile(width), pl.BlockSpec((1, width), lambda step: (0, 0))],
        2 * rows * width * columns * 8,
    )


def product_kernel(count, first, came_first, column, plan, left_refs, right_refs, came_ref, out_ref):
    tile = min(TILE, count)
    for low in range(0, count, tile):
        for left, right, start in plan:
            stop = start + right_refs[right].shape[1]
            total = matmul(left_refs[left][first + low : first + low + tile, :], right_refs[right][...])
            if came_ref is not None:
                total = total + came_ref[came_first + low : came_first + low + tile, column + start : column + stop]
            out_ref[low : low + tile, start:stop] = total


def product(lefts, rights, first, count, came=None, came_first=0, column=0):
    distinct = []
    plan = []
    start = 0
    for which, (left, right) in enumerate(zip(lefts, rights)):
        if not any(left is seen for seen in distinct):
            distinct.append(left)
        plan.append(([left is seen for seen in distinct].index(True), which, start))
        start += right.shape[1]
    n_left, n_right = len(distinct), len(rights)

    def body(*refs):
        came_ref = None if came is None else refs[n_left + n_right]
        product_kernel(
            count, first, came_first, column, plan, refs[:n_left], refs[n_left : n_left + n_right], came_ref, refs[-1]
        )

    ins = [*distinct, *rights] + ([] if came is None else [came])
    vmem = pl.BlockSpec(memory_space=pltpu.VMEM)
    return pl.pallas_call(
        body,
        in_specs=[vmem] * len(ins),
        out_specs=vmem,
        out_shape=shaped(count, start, F32),
        cost_estimate=pl.CostEstimate(
            flops=2 * count * lefts[0].shape[1] * start // COST, bytes_accessed=1024, transcendentals=0
        ),
        compiler_params=pltpu.CompilerParams(vmem_limit_bytes=10 * MIB),
    )(*ins)


def products_kernel(left_of, n_left, *refs):
    lefts, rights, out_ref = refs[:n_left], refs[n_left:-1], refs[-1]
    start = 0
    for left, right in zip(left_of, rights):
        stop = start + right.shape[1]
        out_ref[:, start:stop] = matmul(lefts[left][...], right[...])
        start = stop


def products(lefts, left_of, rights):
    rows, depth = lefts[0].shape
    columns = sum(right.shape[1] for right in rights)
    return call(
        functools.partial(products_kernel, left_of, len(lefts)),
        (rows // TILE,),
        (*lefts, *rights),
        [row_tile(depth)] * len(lefts) + [whole(right) for right in rights],
        shaped(rows, columns, F32),
        row_tile(columns),
        2 * rows * depth * columns,
    )


def flip_kernel(array_ref, *refs):
    out_ref = refs[-1]
    for low in range(0, array_ref.shape[1], PAIR):
        values = array_ref[:, low : low + PAIR].astype(F32)
        if len(refs) == 2:
            values = values * refs[0][...]
        out_ref[low : low + PAIR, :] = values.T.astype(BF16)


def flip(array, live=None):
    rows, width = array.shape
    lives = () if live is None else (live,)
    vmem = pl.BlockSpec(memory_space=pltpu.VMEM)
    return pl.pallas_call(
        flip_kernel,
        out_shape=shaped(width, rows),
        in_specs=[vmem] * (1 + len(lives)),
        out_specs=vmem,
        cost_estimate=pl.CostEstimate(flops=1024, bytes_accessed=1024, transcendentals=0),
        compiler_params=pltpu.CompilerParams(vmem_limit_bytes=10 * MIB),
    )(array, *lives)


def turn_kernel(near_first, place_ref, array_ref, *refs):
    out_ref, turned = refs[-2:]
    core, chip = place_ref[0] % 2, place_ref[0] // 2
    part = out_ref.shape[1] // 8
    for step in range(8):
        high, middle_bit, low = step // 4, (step // 2) % 2, step % 2
        across, near, far = (low, high, middle_bit) if near_first else (high, middle_bit, low)
        block = chip ^ (far * 4 + near * 2 + across)
        values = array_ref[:, pl.ds(pl.multiple_of(block * 2 * part, 2 * part), 2 * part)].astype(F32)
        if len(refs) == 3:
            values = values * refs[0][...]
        turned[...] = values.T
        rows = slice(step * part, (step + 1) * part)
        out_ref[0, rows, :] = turned[pl.ds(pl.multiple_of(core * part, part), part), :].astype(BF16)
        out_ref[1, rows, :] = turned[pl.ds(pl.multiple_of((1 - core) * part, part), part), :].astype(BF16)


def turn(array, place, near_first=False, live=None):
    rows, width = array.shape
    lives = () if live is None else (live,)
    vmem = pl.BlockSpec(memory_space=pltpu.VMEM)
    out = pl.pallas_call(
        functools.partial(turn_kernel, near_first),
        out_shape=jax.ShapeDtypeStruct((2, width // 2, rows), BF16),
        in_specs=[pl.BlockSpec(memory_space=pltpu.SMEM)] + [vmem] * (1 + len(lives)),
        out_specs=vmem,
        scratch_shapes=[pltpu.VMEM((width // 8, rows), F32)],
        cost_estimate=pl.CostEstimate(flops=1024, bytes_accessed=1024, transcendentals=0),
        compiler_params=pltpu.CompilerParams(vmem_limit_bytes=10 * MIB),
    )(place, array, *lives)
    return out.reshape(width, rows)


CORE, ACROSS_X, NEAR_Z, FAR_Z = 1, 2, 4, 8


def hold(*trees):
    return lax.optimization_barrier(trees)


def swap_dp(array, bit, size=16):
    return lax.ppermute(array, "dp", [(place, place ^ bit) for place in range(size)])


def swap_tensor(array):
    return lax.ppermute(array, "tensor", [(0, 1), (1, 0)])


def cut_kernel(count, place_ref, *refs):
    out_ref = refs[-1]
    part = refs[0].shape[0]
    for which in range(count):
        out_ref[which * part : (which + 1) * part, :] = refs[which][...].astype(F32)


def cut(weights, place, parts, flips=(0,)):
    rows, columns = weights[0].shape
    part = rows // parts
    count = len(weights) * len(flips)
    specs = [
        pl.BlockSpec((part, columns), lambda step, ref, bits=bits: (ref[0] ^ bits, 0))
        for bits in flips
        for _ in weights
    ]
    return pl.pallas_call(
        functools.partial(cut_kernel, count),
        out_shape=shaped(count * part, columns, F32),
        grid_spec=pltpu.PrefetchScalarGridSpec(
            num_scalar_prefetch=1,
            grid=(1,),
            in_specs=specs,
            out_specs=pl.BlockSpec((count * part, columns), lambda step, ref: (0, 0)),
        ),
        cost_estimate=pl.CostEstimate(flops=1024, bytes_accessed=1024, transcendentals=0),
        compiler_params=pltpu.CompilerParams(vmem_limit_bytes=20 * MIB),
    )(place, *(list(weights) * len(flips)))


def spread_kernel(wide_ref, *outs):
    part = outs[0].shape[0] // 2
    for place in range(2):
        for which, out in enumerate(outs):
            start = (place * len(outs) + which) * part
            out[place * part : (place + 1) * part, :] = wide_ref[start : start + part, :].astype(BF16)


def spread(wide, count):
    rows, columns = wide.shape
    return call(
        spread_kernel,
        (8,),
        (wide,),
        [row_tile(columns, rows // 8)],
        [shaped(rows // count, columns)] * count,
        [row_tile(columns, rows // 8 // count)] * count,
        1024,
    )


def place_kernel(count, place_ref, *refs):
    pieces, outs = refs[:8], refs[8:]
    place = place_ref[0]
    part = outs[0].shape[0] // 8
    for index in range(8):
        target = place ^ index
        for which in range(count):
            outs[which][pl.ds(pl.multiple_of(target * part, part), part), :] = pieces[index][
                which * part : (which + 1) * part, :
            ].astype(BF16)


def put(pieces, count, place):
    height, columns = pieces[0].shape
    rows = 8 * height // count
    once = dict(pipeline_mode=pl.Buffered(1))
    return pl.pallas_call(
        functools.partial(place_kernel, count),
        out_shape=[shaped(rows, columns)] * count,
        grid_spec=pltpu.PrefetchScalarGridSpec(
            num_scalar_prefetch=1,
            grid=(1,),
            in_specs=[pl.BlockSpec((height, columns), lambda step, ref: (0, 0), **once)] * 8,
            out_specs=[pl.BlockSpec((rows, columns), lambda step, ref: (0, 0), **once)] * count,
        ),
        cost_estimate=pl.CostEstimate(flops=1024, bytes_accessed=1024, transcendentals=0),
        compiler_params=pltpu.CompilerParams(vmem_limit_bytes=20 * MIB),
    )(place, *pieces)


def cast_kernel(wide_ref, out_ref):
    out_ref[...] = wide_ref[...].astype(BF16)


def cast_weight(wide):
    rows, columns = wide.shape
    spec = pl.BlockSpec((rows // 8, columns), lambda row: (row, 0))
    return pl.pallas_call(
        cast_kernel, grid=(8,), out_shape=jax.ShapeDtypeStruct(wide.shape, BF16), in_specs=[spec], out_specs=spec
    )(wide)


def relative_rows(array, dp_place, order):
    blocks = array.reshape(2, 2, 2, 2, array.shape[0] // 16, array.shape[1])
    for axis, bit in enumerate((FAR_Z, NEAR_Z, ACROSS_X, CORE)):
        blocks = jnp.where((dp_place & bit) > 0, jnp.flip(blocks, axis), blocks)
    axes = {FAR_Z: 0, NEAR_Z: 1, ACROSS_X: 2, CORE: 3}
    return blocks.transpose([axes[bit] for bit in order] + [4, 5]).reshape(array.shape)


ORDER_X = (CORE, ACROSS_X, NEAR_Z, FAR_Z)
ORDER_Z = (CORE, NEAR_Z, FAR_Z, ACROSS_X)


class Scatter:
    def __init__(self, lefts, rights, order, came, column):
        self.order, self.stage = order, 1
        part = lefts[0].shape[0] // 4
        self.send = product(lefts, rights, part, part, came, part, column)
        self.kept = product(lefts, rights, 0, part, came, 0, column)

    def go(self):
        self.came = swap_dp(self.send, self.order[self.stage])
        self.stage += 1

    def step(self):
        half = self.kept.shape[0] // 2
        self.send = self.kept[half:] + self.came[half:]
        self.kept = self.kept[:half] + self.came[:half]
        self.go()

    def total(self):
        return self.kept + self.came


def scatter_vector(vector, dp_place):
    kept = relative_rows(vector, dp_place, ORDER_X)
    for bit in ORDER_X:
        half = kept.shape[0] // 2
        kept = kept[:half] + swap_dp(kept[half:], bit)
    return kept


def rates_of(side, local_heads):
    head_ids = jnp.arange(local_heads)
    return tuple(
        jnp.exp2(-8.0 * ((which * local_heads + head_ids).astype(F32) + 1.0) / HEADS)
        for which in (side, 1 - side)
    )


def forward_half(hidden, live, weights, rates):
    parts = project(hidden, live, weights)
    q, sq, k, sk, v, gate = parts
    attended, mixed = attend(q, k, v, gate, rates)
    return (*parts, attended, rates), mixed


def shards_plain(
    inputs, lengths, gain_attn, w_query, w_key, w_value, w_gate_attn, w_out, gain_ffn, w_gate, w_up, w_down, cotangent
):
    own = (w_query, w_key, w_value, w_gate_attn, w_out, w_gate, w_up, w_down)
    others = [cast_weight(swap_tensor(weight.astype(F32))) for weight in own]
    rates = rates_of(lax.axis_index("tensor"), w_query.shape[1] // HEAD_DIM)
    positions = jnp.arange(inputs.shape[0], dtype=jnp.int32)
    live = (positions < lengths[0]).astype(F32)[:, None]
    gain_one, gain_two = gain_attn.reshape(1, -1), gain_ffn.reshape(1, -1)
    out_grad = (live * cotangent.astype(F32)).astype(BF16)
    hidden_one = first_norm(inputs, gain_one)
    half_a, mixed_a = forward_half(hidden_one, live, own[:4], rates[0])
    half_b, mixed_b = forward_half(hidden_one, live, others[:4], rates[1])
    residual, hidden_two, glu, gate_grad, up_grad, branch, back = middle(
        inputs, live, cotangent, (mixed_a, mixed_b), (w_out, others[4]), gain_two, own[5:]
    )
    result, mid_grad, attn_out_grad, gain_two_grad = middle_back(
        residual, hidden_two, live, cotangent, branch, back, gain_two, (others[5], others[6], others[7].T)
    )
    open_a, gate_a = open_back(half_a, attn_out_grad, w_out)
    open_b, gate_b = open_back(half_b, attn_out_grad, others[4])
    back_a = (*attend_back(half_a, open_a), gate_a)
    back_b = (*attend_back(half_b, open_b), gate_b)
    input_grad, gain_one_grad = first_back(
        inputs, mid_grad, gain_one, (*back_a, *back_b), (*own[:4], *others[:4])
    )
    pairs = [(hidden_one, grad) for grad in back_a]
    pairs += [(attn_out_grad, mixed_a), (hidden_two, gate_grad), (hidden_two, up_grad), (out_grad, glu)]
    sums = [
        lax.psum_scatter(matmul(left.T, right), "dp", scatter_dimension=0, tiled=True) for left, right in pairs
    ]
    gains = [lax.psum_scatter(grad[0], "dp", scatter_dimension=0, tiled=True) for grad in (gain_one_grad, gain_two_grad)]
    return (result, input_grad, gains[0], *sums[:4], sums[4].T, gains[1], sums[5], sums[6], sums[7].T)


def shards_here(
    inputs, lengths, gain_attn, w_query, w_key, w_value, w_gate_attn, w_out, gain_ffn, w_gate, w_up, w_down, cotangent
):
    seq_rows = inputs.shape[0]
    side = lax.axis_index("tensor")
    dp_place = lax.axis_index("dp")
    place = (dp_place % 8).reshape(1)
    rates = rates_of(side, w_query.shape[1] // HEAD_DIM)
    positions = jnp.arange(seq_rows, dtype=jnp.int32)
    live = (positions < lengths[0]).astype(F32)[:, None]
    gain_one = gain_attn.reshape(1, -1)
    gain_two = gain_ffn.reshape(1, -1)

    proj = (w_query, w_key, w_value, w_gate_attn)
    whole_place = dp_place.reshape(1)
    y1 = swap_tensor(cut(proj, place, 8))
    features = w_down.shape[1] // 16
    down_piece = lax.dynamic_slice_in_dim(w_down, dp_place * features, features, 1).T
    glu_cut = jnp.concatenate([cut((w_gate, w_up), whole_place, 16), down_piece.astype(F32)], axis=0)
    y2_cut, out_cut = cut(proj, place ^ 6, 8), cut((w_out,), place, 8, (0, 6))
    hidden_one = first_norm(inputs, gain_one)
    parts = project(hidden_one, live, proj)

    y1, parts, glu_cut, out = hold(y1, parts, glu_cut, out_cut)
    out = swap_tensor(out)
    x1, z1, y1c = swap_dp(y1, ACROSS_X), swap_dp(y1, NEAR_Z), swap_dp(y1, CORE)
    glu_cut = swap_tensor(glu_cut)
    q, sq, k, sk, v, gate = parts
    attended, mixed_a = attend(q, k, v, gate, rates[0])
    half_a = (*parts, attended, rates[0])
    dy_t = flip(cotangent, live)

    x1, z1, y1c, glu_cut, mixed_a, dy_t, hidden_one, y2, out = hold(
        x1, z1, y1c, glu_cut, mixed_a, dy_t, hidden_one, y2_cut, out
    )
    part = out.shape[0] // 2
    ox, oz = swap_dp(out[:part], ACROSS_X), swap_dp(out[:part], NEAR_Z)
    glu_wide = lax.all_gather(glu_cut, "dp", axis=0, tiled=True)
    y2 = swap_tensor(y2)
    x1c, z1c = swap_dp(x1, CORE), swap_dp(z1, CORE)
    hidden_one_t = turn(hidden_one, whole_place)
    hidden_one_tz = turn(hidden_one, whole_place, near_first=True)

    y2, x1c, z1c, ox, oz, hidden_one_t, hidden_one_tz = hold(y2, x1c, z1c, ox, oz, hidden_one_t, hidden_one_tz)
    y2c = swap_dp(y2, CORE)
    out_c, out_xz = swap_dp(out, CORE), swap_dp(jnp.concatenate([ox, oz], axis=0), CORE)
    proj_b = put((y1, y1c, x1, x1c, z1, z1c, y2, y2c), 4, place)
    parts = project(hidden_one, live, proj_b)

    parts, out_c, out_xz = hold(parts, out_c, out_xz)
    (w_out_b,) = put(
        (out[:part], out_c[:part], ox, out_xz[:part], oz, out_xz[part:], out[part:], out_c[part:]), 1, place
    )
    q, sq, k, sk, v, gate = parts
    attended, mixed_b = attend(q, k, v, gate, rates[1])
    half_b = (*parts, attended, rates[1])

    residual, hidden_two, glu, gate_grad, up_grad, branch, back = middle(
        inputs, live, cotangent, (mixed_a, mixed_b), (w_out, others[4]), gain_two, own[5:]
    )
    result, mid_grad, attn_out_grad, gain_two_grad = middle_back(
        residual, hidden_two, live, cotangent, branch, back, gain_two, (others[5], others[6], others[7].T)
    )
    open_a, gate_a = open_back(half_a, attn_out_grad, w_out)
    open_b, gate_b = open_back(half_b, attn_out_grad, others[4])
    back_a = (*attend_back(half_a, open_a), gate_a)
    back_b = (*attend_back(half_b, open_b), gate_b)
    input_grad, gain_one_grad = first_back(
        inputs, mid_grad, gain_one, (*back_a, *back_b), (*own[:4], *others[:4])
    )
    pairs = [(hidden_one, grad) for grad in back_a]
    pairs += [(attn_out_grad, mixed_a), (hidden_two, gate_grad), (hidden_two, up_grad), (out_grad, glu)]
    sums = [
        lax.psum_scatter(matmul(left.T, right), "dp", scatter_dimension=0, tiled=True) for left, right in pairs
    ]
    gains = [lax.psum_scatter(grad[0], "dp", scatter_dimension=0, tiled=True) for grad in (gain_one_grad, gain_two_grad)]
    return (result, input_grad, gains[0], *sums[:4], sums[4].T, gains[1], sums[5], sums[6], sums[7].T)


def shards_here(
    inputs, lengths, gain_attn, w_query, w_key, w_value, w_gate_attn, w_out, gain_ffn, w_gate, w_up, w_down, cotangent
):
    seq_rows = inputs.shape[0]
    side = lax.axis_index("tensor")
    dp_place = lax.axis_index("dp")
    place = (dp_place % 8).reshape(1)
    rates = rates_of(side, w_query.shape[1] // HEAD_DIM)
    positions = jnp.arange(seq_rows, dtype=jnp.int32)
    live = (positions < lengths[0]).astype(F32)[:, None]
    gain_one = gain_attn.reshape(1, -1)
    gain_two = gain_ffn.reshape(1, -1)

    proj = (w_query, w_key, w_value, w_gate_attn)
    whole_place = dp_place.reshape(1)
    y1 = swap_tensor(cut(proj, place, 8))
    features = w_down.shape[1] // 16
    down_piece = lax.dynamic_slice_in_dim(w_down, dp_place * features, features, 1).T
    glu_cut = jnp.concatenate([cut((w_gate, w_up), whole_place, 16), down_piece.astype(F32)], axis=0)
    y2_cut, out_cut = cut(proj, place ^ 6, 8), cut((w_out,), place, 8, (0, 6))
    hidden_one = first_norm(inputs, gain_one)
    parts = project(hidden_one, live, proj)

    y1, parts, glu_cut, out = hold(y1, parts, glu_cut, out_cut)
    out = swap_tensor(out)
    x1, z1, y1c = swap_dp(y1, ACROSS_X), swap_dp(y1, NEAR_Z), swap_dp(y1, CORE)
    glu_cut = swap_tensor(glu_cut)
    q, sq, k, sk, v, gate = parts
    attended, mixed_a = attend(q, k, v, gate, rates[0])
    half_a = (*parts, attended, rates[0])
    dy_t = flip(cotangent, live)

    x1, z1, y1c, glu_cut, mixed_a, dy_t, hidden_one, y2, out = hold(
        x1, z1, y1c, glu_cut, mixed_a, dy_t, hidden_one, y2_cut, out
    )
    part = out.shape[0] // 2
    ox, oz = swap_dp(out[:part], ACROSS_X), swap_dp(out[:part], NEAR_Z)
    glu_wide = lax.all_gather(glu_cut, "dp", axis=0, tiled=True)
    y2 = swap_tensor(y2)
    x1c, z1c = swap_dp(x1, CORE), swap_dp(z1, CORE)
    hidden_one_t = turn(hidden_one, whole_place)
    hidden_one_tz = turn(hidden_one, whole_place, near_first=True)

    y2, x1c, z1c, ox, oz, hidden_one_t, hidden_one_tz = hold(y2, x1c, z1c, ox, oz, hidden_one_t, hidden_one_tz)
    y2c = swap_dp(y2, CORE)
    out_c, out_xz = swap_dp(out, CORE), swap_dp(jnp.concatenate([ox, oz], axis=0), CORE)
    proj_b = put((y1, y1c, x1, x1c, z1, z1c, y2, y2c), 4, place)
    parts = project(hidden_one, live, proj_b)

    parts, out_c, out_xz = hold(parts, out_c, out_xz)
    (w_out_b,) = put(
        (out[:part], out_c[:part], ox, out_xz[:part], oz, out_xz[part:], out[part:], out_c[part:]), 1, place
    )
    q, sq, k, sk, v, gate = parts
    attended, mixed_b = attend(q, k, v, gate, rates[1])
    half_b = (*parts, attended, rates[1])

    mixed_b, out_xz = hold(mixed_b, out_xz)
    (w_out_b,) = put(
        (out[:part], out_c[:part], ox, out_xz[:part], oz, out_xz[part:], out[part:], out_c[part:]), 1, place
    )
    residual, hidden_two, glu, gate_grad, up_grad, branch, back = middle(
        inputs, live, cotangent, (mixed_a, mixed_b), (w_out, w_out_b), gain_two, (w_gate, w_up, w_down)
    )
    wide = products((dy_t, flip(hidden_two)), (0, 1, 1), (glu, gate_grad, up_grad))

    residual, wide = hold(residual, wide)
    units = glu.shape[1]
    ffn_sums = lax.psum_scatter(wide, "dp", scatter_dimension=0, tiled=True)
    result, mid_grad, attn_out_grad, gain_two_grad = middle_back(
        residual, hidden_two, live, cotangent, branch, back, gain_two, spread(glu_wide, 3)
    )

    half = dy_t.shape[0] // 2
    open_a, gate_a = open_back(half_a, attn_out_grad, w_out)
    attn_out_grad_t = turn(attn_out_grad, whole_place, near_first=True)
    lefts, rights = (attn_out_grad_t, hidden_one_tz), (mixed_a, gate_a)
    came = swap_dp(product(lefts, rights, half, half), CORE)

    open_a, came, attn_out_grad = hold(open_a, came, attn_out_grad)
    second = Scatter(lefts, rights, ORDER_Z, came, 0)
    second.go()
    own = attend_back(half_a, open_a)

    own, attn_out_grad = hold(own, attn_out_grad)
    lefts = (hidden_one_t,) * 3
    came = swap_dp(product(lefts, own, half, half), CORE)
    open_b, gate_b = open_back(half_b, attn_out_grad, w_out_b)

    open_b, came = hold(open_b, came)
    first = Scatter(lefts, own, ORDER_X, came, 0)
    first.go()
    other = attend_back(half_b, open_b)

    own, other = (*own, gate_a), (*other, gate_b)
    input_grad, gain_one_grad = first_back(inputs, mid_grad, gain_one, (*own, *other), (*proj, *proj_b))

    input_grad, first.came, second.came, gain_one_grad = hold(input_grad, first.came, second.came, gain_one_grad)
    first.step()
    second.step()
    first.came, second.came = hold(first.came, second.came)
    first.step()
    second.step()
    gains = scatter_vector(jnp.concatenate([gain_one_grad, gain_two_grad], axis=0).T, dp_place)
    first_sum, second_sum = first.total(), second.total()
    first_sum, second_sum, ffn_sums = hold(first_sum, second_sum, ffn_sums)
    width = w_query.shape[1]
    return (
        result,
        input_grad,
        gains[:, 0],
        first_sum[:, :width],
        first_sum[:, width : 2 * width],
        first_sum[:, 2 * width :],
        second_sum[:, width:],
        second_sum[:, :width].T,
        gains[:, 1],
        ffn_sums[:, units : 2 * units],
        ffn_sums[:, 2 * units :],
        ffn_sums[:, :units].T,
    )


def solution(mesh):
    placed = (
        P("dp", None),
        P("dp"),
        P(),
        P(None, "tensor"),
        P(None, "tensor"),
        P(None, "tensor"),
        P(None, "tensor"),
        P("tensor", None),
        P(),
        P(None, "tensor"),
        P(None, "tensor"),
        P("tensor", None),
        P("dp", None),
    )
    return jax.shard_map(
        shards_here if mesh.shape["dp"] == 16 else shards_plain,
        mesh=mesh,
        in_specs=placed,
        out_specs=(
            P("dp", None),
            P("dp", None),
            P("dp"),
            P("dp", "tensor"),
            P("dp", "tensor"),
            P("dp", "tensor"),
            P("dp", "tensor"),
            P("tensor", "dp"),
            P("dp"),
            P("dp", "tensor"),
            P("dp", "tensor"),
            P("tensor", "dp"),
        ),
        check_vma=False,
    )
```
